32 devices in a mesh: copies: 2 (over y), dom: 4 (over z), mesh: 2 (over core), sub: 2 (over x).
Axes of the slice: x: 2, y: 2, z: 4, core: 2. Of those that a mesh axis runs over, the one named last changes fastest.
Arguments:
- modes_in: float32 [2, 32, 128, 256], P('mesh', 'copies', 'dom', 'sub'), parts along dimension 1, may hold values from -6 to 6
- stiffness: float32 [4, 128, 256], P(('copies', 'mesh'), 'dom', 'sub'), parts along dimension 0, may hold values from 0.5 to 4
- coupling: bfloat16 [2, 4, 2, 96, 128, 128], P('mesh', 'dom', 'sub'), may hold values from -0.5 to 0.5
- pair_own: int32 [2, 4, 2, 96], P('mesh', 'dom', 'sub'), may hold values from 0 to 31
- pair_peer: int32 [2, 4, 2, 96], P('mesh', 'dom', 'sub'), may hold values from 0 to 3
- pair_slot: int32 [2, 4, 2, 96], P('mesh', 'dom', 'sub'), may hold values from 0 to 7
- send_rows: int32 [2, 4, 2, 4, 8], P('mesh', 'dom', 'sub'), may hold values from 0 to 31
Outputs:
- modes_out: float32 [2, 32, 128, 256], P('mesh', 'copies', 'dom', 'sub'), parts along dimension 1
The draws below stay inside these ranges and needn't reach their ends.
There are 2 independent parts, one for each index of `copies`. The reference program is written for one: setup_inputs(seed, part) draws one part's arguments, and reference() takes and returns one part's arrays. A program takes and returns all parts, laid end to end along the dimension named above; an argument that names none is the same for every part. Nothing has to cross between parts.
All inputs are finite; a program needn't handle non-finite values.
Results may differ from the reference program's by a relative error of at most 0.0012.
Values may be sent and summed in bfloat16 or wider, within the bound.
No kernel may reach another device: no remote copies, remote signals or barrier semaphores. Data moves between devices by JAX's collectives and lax.ppermute only.
A program may use at most 64 MiB of HBM per device.

```python
import math
import jax
import jax.numpy as jnp
from jax import lax

MODES = 16
TILE = 128
CX = 32
PAIRS_DEV = 96
CAP = 8
DOMS = 4
SUBS = 2
NX = 128
NY = 256


def set_ends(values, key, smallest, top_value):
    dims = values.shape
    spot = [jax.random.randint(jax.random.fold_in(key, axis), (), 0, dims[axis]) for axis in range(len(dims))]
    values = values.at[tuple(spot)].set(smallest)
    longest = dims.index(max(dims))
    spot[longest] = (spot[longest] + 1) % dims[longest]
    return values.at[tuple(spot)].set(top_value)


def block_levels(own_key, dims, shards, smallest, top_value):
    gain = 1.0
    for axis_at, blocks in shards:
        steps = jax.random.uniform(jax.random.fold_in(jax.random.fold_in(own_key, 6), axis_at), (blocks,), jnp.float32, smallest / len(shards), top_value / len(shards))
        gain = gain * jnp.repeat(jnp.exp(steps), dims[axis_at] // blocks).reshape((-1,) + (1,) * (len(dims) - 1 - axis_at))
    return gain


def noise(own_key, shape, spread, bound, pieces=(), kind=jnp.bfloat16):
    entries = jax.random.normal(own_key, shape, jnp.float32) * spread
    if len(pieces) > 0:
        entries = block_levels(own_key, shape, pieces, -0.22, 0.18) * entries
    return jnp.clip(entries, min=-bound, max=bound).astype(kind)


def setup_inputs(seed: int = 0, part: int = 0) -> dict:
    seeds = jax.random.split(jax.random.key(seed), 8)
    part_keys = jax.random.split(jax.random.fold_in(seeds[7], part), 8)
    return {
        "modes_in": noise(part_keys[0], (2, MODES, NX, NY), 1.0, 6.0, ((0, 2), (2, 4), (3, 2)), jnp.float32),
        "stiffness": jnp.clip(jnp.exp(math.log(4.0) - 2.0794415 * jax.random.uniform(part_keys[1], (2, NX, NY), jnp.float32) ** block_levels(part_keys[1], (2, NX, NY), ((0, 2), (1, 4), (2, 2)), -0.2, 0.2)), 0.5, 4.0),
        "coupling": noise(seeds[2], (2, DOMS, SUBS, PAIRS_DEV, TILE, TILE), TILE ** -0.5, 0.5, ((0, 2), (1, 4), (2, 2))),
        "pair_own": set_ends(jax.random.randint(seeds[3], (2, DOMS, SUBS, PAIRS_DEV), 0, CX), jax.random.fold_in(seeds[3], 1), 0, CX - 1).astype(jnp.int32),
        "pair_peer": set_ends(jax.random.randint(seeds[4], (2, DOMS, SUBS, PAIRS_DEV), 0, DOMS), jax.random.fold_in(seeds[4], 1), 0, DOMS - 1).astype(jnp.int32),
        "pair_slot": set_ends(jax.random.randint(seeds[5], (2, DOMS, SUBS, PAIRS_DEV), 0, CAP), jax.random.fold_in(seeds[5], 1), 0, CAP - 1).astype(jnp.int32),
        "send_rows": set_ends(jax.random.randint(seeds[6], (2, DOMS, SUBS, DOMS, CAP), 0, CX), jax.random.fold_in(seeds[6], 1), 0, CX - 1).astype(jnp.int32),
    }


helm_shift = 1.0
neighbours = ((1, 0), (-1, 0), (0, 1), (0, -1))


def stencil(values, stiff, shift):
    size_x = values.shape[1]
    size_y = values.shape[2]
    value_pad = jnp.pad(values, ((0, 0), (1, 1), (1, 1)))
    stiff_pad = jnp.pad(stiff, ((1, 1), (1, 1)))
    result = -shift * values
    for spacing_horizontal, step_y in neighbours:
        near_value = value_pad[:, 1 + spacing_horizontal:1 + spacing_horizontal + size_x, 1 + step_y:1 + step_y + size_y]
        near_stiff = stiff_pad[1 + spacing_horizontal:1 + spacing_horizontal + size_x, 1 + step_y:1 + step_y + size_y]
        result = result + 0.5 * (stiff + near_stiff) * (values - near_value)
    return result


def reference(modes_in, stiffness, coupling, pair_own, pair_peer, pair_slot, send_rows):
    stencil_part = jnp.stack([stencil(modes_in[0], stiffness[0], 0.0),
                              stencil(modes_in[1], stiffness[1], helm_shift)])
    tiles = modes_in.astype(jnp.bfloat16)
    tiled = tiles.reshape(2, MODES, DOMS, CX, SUBS, TILE).transpose(0, 2, 4, 3, 1, 5)
    sub_range = jnp.arange(SUBS, dtype=jnp.int32)[:, None]

    def holder(index):
        half = index // DOMS
        region_index = index % DOMS
        other = 1 - half
        block_groups = coupling[half, region_index].astype(jnp.float32)
        own_rows = pair_own[half, region_index]
        peers = pair_peer[half, region_index]
        slots = pair_slot[half, region_index]
        remote_rows = send_rows[other][peers, sub_range, region_index, slots]
        resident_tile_set = tiled[half, region_index][sub_range, own_rows].astype(jnp.float32)
        foreign_tile_set = tiled[other][peers, sub_range, remote_rows].astype(jnp.float32)
        self_contributions = jnp.einsum('dxug,dxvg->dxuv', foreign_tile_set, block_groups, precision=lax.Precision.HIGHEST)
        return_contributions = jnp.einsum('ugtn,ugnw->ugtw', resident_tile_set, block_groups, precision=lax.Precision.HIGHEST)
        return self_contributions, return_contributions, remote_rows

    holders = jnp.arange(2 * DOMS, dtype=jnp.int32)
    self_contributions, return_contributions, remote_rows = lax.map(holder, holders)
    shape_pairs = (2 * DOMS, SUBS, PAIRS_DEV)
    half_index = jnp.broadcast_to((holders // DOMS)[:, None, None], shape_pairs)
    domain_index = jnp.broadcast_to((holders % DOMS)[:, None, None], shape_pairs)
    sub_index = jnp.broadcast_to(jnp.arange(SUBS, dtype=jnp.int32)[None, :, None], shape_pairs)
    contrib = jnp.zeros((2, DOMS, SUBS, CX, MODES, TILE), jnp.float32)
    contrib = contrib.at[half_index, domain_index, sub_index, pair_own.reshape(shape_pairs)].add(self_contributions)
    contrib = contrib.at[1 - half_index, pair_peer.reshape(shape_pairs), sub_index, remote_rows].add(return_contributions)
    coupled = contrib.transpose(0, 4, 1, 3, 2, 5).reshape(2, MODES, NX, NY)
    return stencil_part - coupled
```

```python
import functools

import jax
import jax.numpy as jnp
from jax import lax
from jax.experimental import pallas as pl
from jax.experimental.pallas import tpu as pltpu
from jax.sharding import PartitionSpec as P

helm_shift = 1.0
PIECES = 4
CHUNK = 16
LANES = 64
VMEM = pl.BlockSpec(memory_space=pltpu.VMEM)
HBM = pl.BlockSpec(memory_space=pltpu.HBM)


def pieces(x):
    high = x.astype(jnp.bfloat16)
    rest = x - high.astype(jnp.float32)
    middle = rest.astype(jnp.bfloat16)
    low = (rest - middle.astype(jnp.float32)).astype(jnp.bfloat16)
    return high, middle, low


def whole(high, middle, low):
    f = jnp.float32
    return high.astype(f) + (middle.astype(f) + low.astype(f))


def load(sources, targets, sems):
    copies = [pltpu.make_async_copy(a, b, sems.at[i]) for i, (a, b) in enumerate(zip(sources, targets))]
    for copy in copies:
        copy.start()
    return copies


def before(doms, slots, rows, own_in, peer_in, slot_in, send_in, modes_in, stiff_in, coupling, *refs):
    outs, (edges, column, blocks) = refs[:doms], refs[doms : doms + 3]
    own, peer, slot, send, modes, stiff, tiles, sums, sems, block_sems = refs[doms + 3 :]
    sources = (own_in, peer_in, slot_in, send_in, modes_in, stiff_in)
    copies = load(sources, (own, peer, slot, send, modes, stiff), sems)
    parts = [pl.ds(i, CHUNK) for i in range(0, blocks.shape[0], CHUNK)]
    block_copies = load([coupling.at[0, 0, 0, part] for part in parts], [blocks.at[part] for part in parts], block_sems)
    d = lax.axis_index("dom")
    count, cells = tiles.shape[1:]
    sums[...] = jnp.zeros_like(sums)
    for copy in copies:
        copy.wait()
    for r in range(rows):
        tiles[r] = modes[pl.ds(r, count, stride=rows), :].astype(jnp.bfloat16)

    def edge_tiles(target, first, row):
        edge = modes[pl.ds(row, count, stride=rows), :]
        for i, piece in enumerate(pieces(edge)):
            target[first + i] = piece
        edge = jnp.broadcast_to(stiff[0, pl.ds(row, 1), :], edge.shape)
        line = lax.broadcasted_iota(jnp.int32, edge.shape, 0)
        high, middle, low = (p.astype(jnp.float32) for p in pieces(edge))
        mixed = jnp.where(line == 0, high, jnp.where(line == 1, middle, low))
        target[first + 3] = mixed.astype(jnp.bfloat16)

    even = d % 2 == 0
    if doms > 1:
        edge_tiles(outs[1], 2 * slots, jnp.where(even, rows - 1, 0))
    edge_tiles(edges, 0, jnp.where(even, 0, rows - 1))
    for k in range(doms):
        for j in range(slots):
            outs[k][j] = tiles[send[0, 0, 0, d ^ k, j]]
    lane = lax.broadcasted_iota(jnp.int32, (rows, cells), 1)
    packed = jnp.zeros((rows, cells), jnp.float32)
    for m in range(count + 1):
        here = stiff[0] if m == count else modes[m * rows : (m + 1) * rows, :]
        packed = jnp.where(lane == m, here[:, :1], packed)
        packed = jnp.where(lane == LANES + m, here[:, -1:], packed)
    column[...] = packed
    for c, copy in enumerate(block_copies):
        copy.wait()
        for p in range(c * CHUNK, (c + 1) * CHUNK):
            term = jnp.dot(tiles[own[0, 0, 0, p]], blocks[p], preferred_element_type=jnp.float32)
            sums[peer[0, 0, 0, p] * slots + slot[0, 0, 0, p]] += term
    for k in range(doms):
        for j in range(slots):
            outs[k][slots + j] = sums[(d ^ k) * slots + j].astype(jnp.bfloat16)


def pick(slots, arrived, halo):
    halo[...] = arrived[2 * slots : 2 * slots + PIECES]


def after(doms, slots, subs, rows, own_in, peer_in, slot_in, send_in, modes_in, stiff_in, blocks, near, far, *refs):
    arrived, columns, out = refs[:doms], refs[doms:-11], refs[-11]
    own, peer, slot, send, modes, stiff, foreign, total, back, sems = refs[-10:]
    sources = (own_in, peer_in, slot_in, send_in, modes_in, stiff_in)
    copies = load(sources, (own, peer, slot, send, modes, stiff), sems)
    d = lax.axis_index("dom")
    s = lax.axis_index("sub")
    shift = helm_shift * lax.axis_index("mesh").astype(jnp.float32)
    count, cells = foreign.shape[1:]
    total[...] = jnp.zeros_like(total)
    for k in range(doms):
        for j in range(slots):
            foreign[(d ^ k) * slots + j] = arrived[k][j]
            back[(d ^ k) * slots + j] = arrived[k][slots + j].astype(jnp.float32)
    for copy in copies:
        copy.wait()
    for g in range(doms):
        for j in range(slots):
            total[send[0, 0, 0, g, j]] += back[g * slots + j]
    for p in range(blocks.shape[0]):
        term = lax.dot_general(
            foreign[peer[0, 0, 0, p] * slots + slot[0, 0, 0, p]],
            blocks[p],
            (((1,), (1,)), ((), ())),
            preferred_element_type=jnp.float32,
        )
        total[own[0, 0, 0, p]] += term
    lane = lax.broadcasted_iota(jnp.int32, (rows, cells), 1)
    line = lax.broadcasted_iota(jnp.int32, (rows, cells), 0)
    first_lane, last_lane = lane == 0, lane == cells - 1
    first_line, last_line = line == 0, line == rows - 1
    if subs == 1:
        left = right = jnp.zeros(lane.shape, jnp.float32)
    elif subs == 2:
        left, right = jnp.where(s == 1, columns[0][...], 0.0), jnp.where(s == 0, columns[0][...], 0.0)
    else:
        left, right = columns[0][...], columns[1][...]

    def around(here, above, below, m):
        return (
            jnp.where(first_line, above, pltpu.roll(here, 1, 0)),
            jnp.where(last_line, below, pltpu.roll(here, rows - 1, 0)),
            jnp.where(first_lane, left[:, LANES + m : LANES + m + 1], pltpu.roll(here, 1, 1)),
            jnp.where(last_lane, right[:, m : m + 1], pltpu.roll(here, cells - 1, 1)),
        )

    even = d % 2 == 0
    inner = [whole(*(ref[i] for i in range(3))) for ref in (near, far)]
    coefficients = [whole(*(ref[3, i : i + 1] for i in range(3))) for ref in (near, far)]
    above, below = (jnp.where(even, inner[1 - i], inner[i]) for i in range(2))
    stiff_above, stiff_below = (jnp.where(even, coefficients[1 - i], coefficients[i]) for i in range(2))
    weights = [0.5 * (stiff[0] + beside) for beside in around(stiff[0], stiff_above, stiff_below, count)]
    for m in range(count):
        here = modes[m * rows : (m + 1) * rows, :]
        result = -shift * here
        for weight, beside in zip(weights, around(here, above[m : m + 1], below[m : m + 1], m)):
            result = result + weight * (here - beside)
        out[m * rows : (m + 1) * rows, :] = result - total[:, m, :]


def shards(doms, subs, modes_in, stiffness, coupling, pair_own, pair_peer, pair_slot, send_rows):
    _, count, rows, cells = modes_in.shape
    slots, pairs = send_rows.shape[-1], coupling.shape[3]
    flat = modes_in.reshape(count * rows, cells)
    inputs = (pair_own, pair_peer, pair_slot, send_rows, flat, stiffness, coupling)
    *inputs, coupling = [pltpu.with_memory_space_constraint(a, pltpu.HBM) for a in inputs]
    params = pltpu.CompilerParams(vmem_limit_bytes=32 * 1024 * 1024)
    held = [pltpu.SMEM(a.shape, a.dtype) for a in inputs[:4]] + [pltpu.VMEM(a.shape, a.dtype) for a in inputs[4:]]
    like = jax.ShapeDtypeStruct
    *outgoing, edges, column, blocks = pl.pallas_call(
        functools.partial(before, doms, slots, rows),
        out_shape=[like((2 * slots + PIECES * (k == 1), count, cells), jnp.bfloat16) for k in range(doms)]
        + [
            like((PIECES, count, cells), jnp.bfloat16),
            like((rows, cells), jnp.float32),
            like((pairs, cells, cells), jnp.bfloat16),
        ],
        in_specs=[HBM] * 7,
        out_specs=[VMEM] * (doms + 3),
        scratch_shapes=held
        + [
            pltpu.VMEM((rows, count, cells), jnp.bfloat16),
            pltpu.VMEM((doms * slots, count, cells), jnp.float32),
            pltpu.SemaphoreType.DMA((len(inputs),)),
            pltpu.SemaphoreType.DMA((pairs // CHUNK,)),
        ],
        compiler_params=params,
        name="before",
    )(*inputs, coupling)
    order = list(range(doms - 1, 0, -1)) + [0]
    if doms == 4:
        order = [3, 1, 2, 0]
    arrived = {}
    for k in order:
        route = [(2 * d + h, 2 * (d ^ k) + 1 - h) for d in range(doms) for h in range(2)]
        arrived[k] = lax.ppermute(outgoing[k], ("dom", "mesh"), route)
    if subs == 1:
        columns = []
    elif subs == 2:
        columns = [lax.ppermute(column, "sub", [(0, 1), (1, 0)])]
    else:
        columns = [
            lax.ppermute(column, "sub", [(i, i + 1) for i in range(subs - 1)]),
            lax.ppermute(column, "sub", [(i + 1, i) for i in range(subs - 1)]),
        ]
    cuts = [(i, i + 1) for i in range(1, doms - 1, 2)]
    far = lax.ppermute(edges, "dom", cuts + [(j, i) for i, j in cuts])
    near = pl.pallas_call(
        functools.partial(pick, slots),
        out_shape=like((PIECES, count, cells), jnp.bfloat16),
        in_specs=[VMEM],
        out_specs=VMEM,
        compiler_params=params,
        name="pick",
    )(arrived[1])
    near = lax.ppermute(near, "mesh", [(0, 1), (1, 0)])
    out = pl.pallas_call(
        functools.partial(after, doms, slots, subs, rows),
        out_shape=like(flat.shape, jnp.float32),
        in_specs=[HBM] * 6 + [VMEM] * (3 + doms + len(columns)),
        out_specs=VMEM,
        scratch_shapes=held
        + [
            pltpu.VMEM((doms * slots, count, cells), jnp.bfloat16),
            pltpu.VMEM((rows, count, cells), jnp.float32),
            pltpu.VMEM((doms * slots, count, cells), jnp.float32),
            pltpu.SemaphoreType.DMA((len(inputs),)),
        ],
        compiler_params=params,
        name="after",
    )(*inputs, blocks, near, far, *(arrived[k] for k in range(doms)), *columns)
    return out.reshape(modes_in.shape)


def solution(mesh):
    return jax.shard_map(
        functools.partial(shards, mesh.shape["dom"], mesh.shape["sub"]),
        mesh=mesh,
        in_specs=(
            P("mesh", "copies", "dom", "sub"),
            P(("copies", "mesh"), "dom", "sub"),
            P("mesh", "dom", "sub", None, None, None),
            P("mesh", "dom", "sub", None),
            P("mesh", "dom", "sub", None),
            P("mesh", "dom", "sub", None),
            P("mesh", "dom", "sub", None, None),
        ),
        out_specs=P("mesh", "copies", "dom", "sub"),
        check_vma=False,
    )
```

```python
import functools

import jax
import jax.numpy as jnp
from jax import lax
from jax.experimental import pallas as pl
from jax.experimental.pallas import tpu as pltpu
from jax.sharding import PartitionSpec as P

helm_shift = 1.0
PIECES = 3
VMEM = pl.BlockSpec(memory_space=pltpu.VMEM)
ANY = pl.BlockSpec(memory_space=pl.ANY)
HBM = pl.BlockSpec(memory_space=pltpu.HBM)


def has_halo(k):
    return k > 0 and k & (k + 1) == 0


def pieces(x):
    high = x.astype(jnp.bfloat16)
    return high, (x - high.astype(jnp.float32)).astype(jnp.bfloat16)


def whole(high, low):
    return high.astype(jnp.float32) + low.astype(jnp.float32)


def pair_dot(a, b, blocks):
    none = jnp.zeros_like(a)
    rows = jnp.concatenate([jnp.concatenate([a, none], 1), jnp.concatenate([none, b], 1)], 0)
    both = jnp.dot(rows, blocks.reshape(2 * blocks.shape[1], -1), preferred_element_type=jnp.float32)
    return both[: a.shape[0]], both[a.shape[0] :]


def load(sources, targets, sems):
    copies = [pltpu.make_async_copy(a, b, sems.at[i]) for i, (a, b) in enumerate(zip(sources, targets))]
    for copy in copies:
        copy.start()
    return copies


def before(doms, slots, rows, own_in, peer_in, slot_in, send_in, modes_in, stiff_in, coupling, *refs):
    outs, (column, blocks, modes, stiff) = refs[:doms], refs[doms : doms + 4]
    own, peer, slot, send, tiles, sums, sems, block_sems = refs[doms + 4 :]
    sources = (own_in, peer_in, slot_in, send_in, modes_in, stiff_in)
    copies = load(sources, (own, peer, slot, send, modes, stiff), sems)
    half = blocks.shape[0] // 2
    parts = [pl.ds(0, half), pl.ds(half, half)]
    block_copies = load([coupling.at[0, 0, 0, part] for part in parts], [blocks.at[part] for part in parts], block_sems)
    d = lax.axis_index("dom")
    count, cells = tiles.shape[1:]
    sums[...] = jnp.zeros_like(sums)
    for copy in copies:
        copy.wait()
    for r in range(rows):
        tiles[r] = modes[pl.ds(r, count, stride=rows), :].astype(jnp.bfloat16)

    for k in filter(has_halo, range(doms)):
        row = jnp.where(d ^ k > d, rows - 1, 0)
        edge = modes[pl.ds(row, count, stride=rows), :]
        for i, piece in enumerate(pieces(edge)):
            outs[k][2 * slots + i] = piece
        edge = jnp.broadcast_to(stiff[0, pl.ds(row, 1), :], edge.shape)
        line = lax.broadcasted_iota(jnp.int32, edge.shape, 0)
        high, low = (p.astype(jnp.float32) for p in pieces(edge))
        outs[k][2 * slots + 2] = jnp.where(line == 0, high, low).astype(jnp.bfloat16)
    for k in range(doms):
        for j in range(slots):
            outs[k][j] = tiles[send[0, 0, 0, d ^ k, j]]
    lane = lax.broadcasted_iota(jnp.int32, (rows, cells), 1)
    ends = [jnp.zeros((rows, cells), jnp.float32)] * 2
    for m in range(count + 1):
        here = stiff[0] if m == count else modes[m * rows : (m + 1) * rows, :]
        ends = [jnp.where(lane == m, end, packed) for end, packed in zip((here[:, :1], here[:, -1:]), ends)]
    for side in range(2):
        column[side] = ends[side]
    for c, copy in enumerate(block_copies):
        copy.wait()
        for p in range(c * half, (c + 1) * half, 2):
            terms = pair_dot(tiles[own[0, 0, 0, p]], tiles[own[0, 0, 0, p + 1]], blocks[p : p + 2])
            for q, term in zip((p, p + 1), terms):
                sums[peer[0, 0, 0, q] * slots + slot[0, 0, 0, q]] += term
    for k in range(doms):
        for j in range(slots):
            outs[k][slots + j] = sums[(d ^ k) * slots + j].astype(jnp.bfloat16)


def turn(slots, own_in, peer_in, slot_in, send_in, blocks, turned, table, own, peer, slot, send, sems):
    copies = load((own_in, peer_in, slot_in, send_in), (own, peer, slot, send), sems)
    for p in range(blocks.shape[0]):
        turned[p] = blocks[p].T
    for copy in copies:
        copy.wait()
    pairs, (doms, caps) = own.shape[-1], send.shape[-2:]
    table[...] = jnp.zeros_like(table)
    table[0:1, :pairs] = own[0, 0]
    table[1:2, :pairs] = peer[0, 0] * slots + slot[0, 0]
    table[2 : 2 + doms, :caps] = send[0, 0, 0]


def pick(doms, slots, *refs):
    arrived, halo = dict(zip(filter(has_halo, exchange(doms)), refs)), refs[-1]
    d = lax.axis_index("dom")
    halo[...] = jnp.zeros_like(halo)
    for k, ref in arrived.items():
        for side, step in enumerate((-1, 1)):

            @pl.when(d ^ k == d + step)
            def _():
                halo[side] = ref[2 * slots : 2 * slots + PIECES]


def couple(doms, slots, subs, table_in, modes, stiff, turned, *refs):
    arrived, columns = dict(zip(exchange(doms), refs)), refs[doms:-5]
    total, table, foreign, back, sem = refs[-5:]
    rows = stiff.shape[1]
    copy = pltpu.make_async_copy(table_in, table, sem)
    copy.start()
    d = lax.axis_index("dom")
    s = lax.axis_index("sub")
    shift = helm_shift * lax.axis_index("mesh").astype(jnp.float32)
    count, cells = foreign.shape[1:]
    for k in range(doms):
        for j in range(slots):
            foreign[(d ^ k) * slots + j] = arrived[k][j]
            back[(d ^ k) * slots + j] = arrived[k][slots + j].astype(jnp.float32)
    lane = lax.broadcasted_iota(jnp.int32, (rows, cells), 1)
    line = lax.broadcasted_iota(jnp.int32, (rows, cells), 0)
    first_lane, last_lane = lane == 0, lane == cells - 1
    first_line, last_line = line == 0, line == rows - 1
    if subs == 1:
        left = right = jnp.zeros(lane.shape, jnp.float32)
    elif subs == 2:
        left, right = jnp.where(s == 1, columns[0][1], 0.0), jnp.where(s == 0, columns[0][0], 0.0)
    else:
        left, right = columns[0][1], columns[1][0]

    def near_by(here, m):
        return (
            jnp.where(first_line, here, pltpu.roll(here, 1, 0)),
            jnp.where(last_line, here, pltpu.roll(here, rows - 1, 0)),
            jnp.where(first_lane, left[:, m : m + 1], pltpu.roll(here, 1, 1)),
            jnp.where(last_lane, right[:, m : m + 1], pltpu.roll(here, cells - 1, 1)),
        )

    weights = [0.5 * (stiff[0] + near) for near in near_by(stiff[0], count)]
    for m in range(count):
        here = modes[m * rows : (m + 1) * rows, :]
        result = -shift * here
        for weight, near in zip(weights, near_by(here, m)):
            result = result + weight * (here - near)
        total[pl.ds(m, rows, stride=count), :] = result
    copy.wait()

    def subtract(row, term):
        part = pl.ds(pl.multiple_of(row * count, count), count)
        total[part, :] -= term

    for g in range(doms):
        for j in range(slots):
            subtract(table[2 + g, j], back[g * slots + j])
    for p in range(0, turned.shape[0], 2):
        first, second = (foreign[table[1, q]] for q in (p, p + 1))
        for q, term in zip((p, p + 1), pair_dot(first, second, turned[p : p + 2])):
            subtract(table[0, q], term)


def finish(total, modes, stiff, halo, out):
    rows = stiff.shape[1]
    count = total.shape[0] // rows
    for m in range(count):
        out[m * rows : (m + 1) * rows, :] = total[pl.ds(m, rows, stride=count), :]
    for side, row in enumerate((0, rows - 1)):
        here = modes[pl.ds(row, count, stride=rows), :]
        near = whole(halo[side, 0], halo[side, 1])
        weight = 0.5 * (stiff[0, row : row + 1, :] + whole(halo[side, 2, 0:1], halo[side, 2, 1:2]))
        out[pl.ds(row, count, stride=rows), :] = total[row * count : (row + 1) * count, :] + weight * (here - near)


def exchange(doms):
    if doms == 4:
        return [3, 1, 2, 0]
    return list(range(doms))


def shards(doms, subs, modes_in, stiffness, coupling, pair_own, pair_peer, pair_slot, send_rows):
    _, count, rows, cells = modes_in.shape
    slots, pairs = send_rows.shape[-1], coupling.shape[3]
    flat = modes_in.reshape(count * rows, cells)
    inputs = (pair_own, pair_peer, pair_slot, send_rows, flat, stiffness, coupling)
    *inputs, coupling = [pltpu.with_memory_space_constraint(a, pltpu.HBM) for a in inputs]
    params = pltpu.CompilerParams(vmem_limit_bytes=32 * 1024 * 1024)
    like = jax.ShapeDtypeStruct
    indices = inputs[:4]
    *outgoing, column, blocks, modes, stiff = pl.pallas_call(
        functools.partial(before, doms, slots, rows),
        out_shape=[like((2 * slots + PIECES * has_halo(k), count, cells), jnp.bfloat16) for k in range(doms)]
        + [
            like((2, rows, cells), jnp.float32),
            like((pairs, cells, cells), jnp.bfloat16),
            like(flat.shape, jnp.float32),
            like(stiffness.shape, jnp.float32),
        ],
        in_specs=[HBM] * 7,
        out_specs=[VMEM] * (doms + 4),
        scratch_shapes=[pltpu.SMEM(a.shape, a.dtype) for a in indices]
        + [
            pltpu.VMEM((rows, count, cells), jnp.bfloat16),
            pltpu.VMEM((doms * slots, count, cells), jnp.float32),
            pltpu.SemaphoreType.DMA((len(inputs),)),
            pltpu.SemaphoreType.DMA((2,)),
        ],
        compiler_params=params,
        name="before",
    )(*inputs, coupling)
    arrived = {}
    for k in exchange(doms):
        route = [(2 * d + h, 2 * (d ^ k) + 1 - h) for d in range(doms) for h in range(2)]
        arrived[k] = lax.ppermute(outgoing[k], ("dom", "mesh"), route)
    if subs == 1:
        columns = []
    elif subs == 2:
        columns = [lax.ppermute(column, "sub", [(0, 1), (1, 0)])]
    else:
        columns = [
            lax.ppermute(column, "sub", [(i, i + 1) for i in range(subs - 1)]),
            lax.ppermute(column, "sub", [(i + 1, i) for i in range(subs - 1)]),
        ]
    turned, table = pl.pallas_call(
        functools.partial(turn, slots),
        out_shape=[like(blocks.shape, blocks.dtype), like((-(-(2 + doms) // 8) * 8, cells), jnp.int32)],
        in_specs=[HBM] * 4 + [VMEM],
        out_specs=[VMEM] * 2,
        scratch_shapes=[pltpu.VMEM(a.shape, a.dtype) for a in indices] + [pltpu.SemaphoreType.DMA((4,))],
        compiler_params=params,
        cost_estimate=pl.CostEstimate(flops=0, bytes_accessed=8 << 20, transcendentals=0),
        name="turn",
    )(*indices, blocks)
    halo = pl.pallas_call(
        functools.partial(pick, doms, slots),
        out_shape=like((2, PIECES, count, cells), jnp.bfloat16),
        in_specs=[VMEM] * sum(map(has_halo, range(doms))) + [ANY],
        out_specs=VMEM,
        compiler_params=params,
        name="pick",
    )(*(arrived[k] for k in exchange(doms) if has_halo(k)), turned)
    halo = lax.ppermute(halo, "mesh", [(0, 1), (1, 0)])
    total = pl.pallas_call(
        functools.partial(couple, doms, slots, subs),
        out_shape=like((rows * count, cells), jnp.float32),
        in_specs=[VMEM] * (4 + doms + len(columns)),
        out_specs=VMEM,
        scratch_shapes=[
            pltpu.SMEM(table.shape, table.dtype),
            pltpu.VMEM((doms * slots, count, cells), jnp.bfloat16),
            pltpu.VMEM((doms * slots, count, cells), jnp.float32),
            pltpu.SemaphoreType.DMA,
        ],
        compiler_params=params,
        cost_estimate=pl.CostEstimate(flops=0, bytes_accessed=8 << 20, transcendentals=0),
        name="couple",
    )(table, modes, stiff, turned, *(arrived[k] for k in exchange(doms)), *columns)
    out = pl.pallas_call(
        finish,
        out_shape=like(flat.shape, jnp.float32),
        in_specs=[VMEM] * 4,
        out_specs=VMEM,
        compiler_params=params,
        name="finish",
    )(total, modes, stiff, halo)
    return out.reshape(modes_in.shape)


def solution(mesh):
    return jax.shard_map(
        functools.partial(shards, mesh.shape["dom"], mesh.shape["sub"]),
        mesh=mesh,
        in_specs=(
            P("mesh", "copies", "dom", "sub"),
            P(("copies", "mesh"), "dom", "sub"),
            P("mesh", "dom", "sub", None, None, None),
            P("mesh", "dom", "sub", None),
            P("mesh", "dom", "sub", None),
            P("mesh", "dom", "sub", None),
            P("mesh", "dom", "sub", None, None),
        ),
        out_specs=P("mesh", "copies", "dom", "sub"),
        check_vma=False,
    )
```

```python
import functools

import jax
import jax.numpy as jnp
from jax import lax
from jax.experimental import pallas as pl
from jax.experimental.pallas import tpu as pltpu
from jax.sharding import PartitionSpec as P

helm_shift = 1.0
PIECES = 3
SMEM = pl.BlockSpec(memory_space=pltpu.SMEM)
VMEM = pl.BlockSpec(memory_space=pltpu.VMEM)
ANY = pl.BlockSpec(memory_space=pl.ANY)
HBM = pl.BlockSpec(memory_space=pltpu.HBM)


def has_halo(k):
    return k > 0 and k & (k + 1) == 0


def pieces(x):
    high = x.astype(jnp.bfloat16)
    return high, (x - high.astype(jnp.float32)).astype(jnp.bfloat16)


def whole(high, low):
    return high.astype(jnp.float32) + low.astype(jnp.float32)


def pair_dot(a, b, blocks):
    none = jnp.zeros_like(a)
    rows = jnp.concatenate([jnp.concatenate([a, none], 1), jnp.concatenate([none, b], 1)], 0)
    both = jnp.dot(rows, blocks.reshape(2 * blocks.shape[1], -1), preferred_element_type=jnp.float32)
    return both[: a.shape[0]], both[a.shape[0] :]


def load(sources, targets, sems, priority=0):
    copies = [pltpu.make_async_copy(a, b, sems.at[i]) for i, (a, b) in enumerate(zip(sources, targets))]
    for copy in copies:
        copy.start(priority=priority)
    return copies


def before(doms, slots, rows, own_in, peer_in, slot_in, send_in, modes_in, stiff_in, coupling, *refs):
    outs, (column, blocks, modes, stiff) = refs[:doms], refs[doms : doms + 4]
    own, peer, slot, send, tiles, sums, sems, block_sems = refs[doms + 4 :]
    sources = (own_in, peer_in, slot_in, send_in, modes_in, stiff_in)
    copies = load(sources, (own, peer, slot, send, modes, stiff), sems)
    half = blocks.shape[0] // 2
    parts = [pl.ds(0, half), pl.ds(half, half)]
    block_copies = load([coupling.at[0, 0, 0, part] for part in parts], [blocks.at[part] for part in parts], block_sems, 1)
    d = lax.axis_index("dom")
    count, cells = tiles.shape[1:]
    sums[...] = jnp.zeros_like(sums)
    for copy in copies:
        copy.wait()
    for r in range(rows):
        tiles[r] = modes[pl.ds(r, count, stride=rows), :].astype(jnp.bfloat16)

    for k in filter(has_halo, range(doms)):
        row = jnp.where(d ^ k > d, rows - 1, 0)
        edge = modes[pl.ds(row, count, stride=rows), :]
        for i, piece in enumerate(pieces(edge)):
            outs[k][2 * slots + i] = piece
        edge = jnp.broadcast_to(stiff[0, pl.ds(row, 1), :], edge.shape)
        line = lax.broadcasted_iota(jnp.int32, edge.shape, 0)
        high, low = (p.astype(jnp.float32) for p in pieces(edge))
        outs[k][2 * slots + 2] = jnp.where(line == 0, high, low).astype(jnp.bfloat16)
    for k in range(doms):
        for j in range(slots):
            outs[k][j] = tiles[send[0, 0, 0, d ^ k, j]]
    lane = lax.broadcasted_iota(jnp.int32, (rows, cells), 1)
    ends = [jnp.zeros((rows, cells), jnp.float32)] * 2
    for m in range(count + 1):
        here = stiff[0] if m == count else modes[m * rows : (m + 1) * rows, :]
        ends = [jnp.where(lane == m, end, packed) for end, packed in zip((here[:, :1], here[:, -1:]), ends)]
    for side in range(2):
        column[side] = ends[side]
    for c, copy in enumerate(block_copies):
        copy.wait()
        for p in range(c * half, (c + 1) * half, 2):
            terms = pair_dot(tiles[own[0, 0, 0, p]], tiles[own[0, 0, 0, p + 1]], blocks[p : p + 2])
            for q, term in zip((p, p + 1), terms):
                sums[peer[0, 0, 0, q] * slots + slot[0, 0, 0, q]] += term
    for k in range(doms):
        for j in range(slots):
            outs[k][slots + j] = sums[(d ^ k) * slots + j].astype(jnp.bfloat16)


def turn(blocks, turned):
    for p in range(blocks.shape[0]):
        turned[p] = blocks[p].T


def stencil(subs, modes, stiff, *refs):
    columns, total = refs[:-1], refs[-1]
    rows, cells = stiff.shape[1:]
    count = modes.shape[0] // rows
    shift = helm_shift * lax.axis_index("mesh").astype(jnp.float32)
    lane = lax.broadcasted_iota(jnp.int32, (rows, cells), 1)
    line = lax.broadcasted_iota(jnp.int32, (rows, cells), 0)
    first_lane, last_lane = lane == 0, lane == cells - 1
    first_line, last_line = line == 0, line == rows - 1
    s = lax.axis_index("sub")
    if subs == 1:
        left = right = jnp.zeros(lane.shape, jnp.float32)
    elif subs == 2:
        left, right = jnp.where(s == 1, columns[0][1], 0.0), jnp.where(s == 0, columns[0][0], 0.0)
    else:
        left, right = columns[0][1], columns[1][0]

    def near_by(here, m):
        return (
            jnp.where(first_line, here, pltpu.roll(here, 1, 0)),
            jnp.where(last_line, here, pltpu.roll(here, rows - 1, 0)),
            jnp.where(first_lane, left[:, m : m + 1], pltpu.roll(here, 1, 1)),
            jnp.where(last_lane, right[:, m : m + 1], pltpu.roll(here, cells - 1, 1)),
        )

    weights = [0.5 * (stiff[0] + near) for near in near_by(stiff[0], count)]
    for m in range(count):
        here = modes[m * rows : (m + 1) * rows, :]
        result = -shift * here
        for weight, near in zip(weights, near_by(here, m)):
            result = result + weight * (here - near)
        total[pl.ds(m, rows, stride=count), :] = result


def pick(doms, slots, *refs):
    arrived, halo = dict(zip(filter(has_halo, exchange(doms)), refs)), refs[-1]
    d = lax.axis_index("dom")
    halo[...] = jnp.zeros_like(halo)
    for k, ref in arrived.items():
        for side, step in enumerate((-1, 1)):

            @pl.when(d ^ k == d + step)
            def _():
                halo[side] = ref[2 * slots : 2 * slots + PIECES]


def couple(doms, slots, own, peer, slot, send, turned, *refs):
    arrived, (_, total, foreign, back) = dict(zip(exchange(doms), refs)), refs[doms:]
    count = foreign.shape[1]
    d = lax.axis_index("dom")
    for k in range(doms):
        for j in range(slots):
            foreign[(d ^ k) * slots + j] = arrived[k][j]
            back[(d ^ k) * slots + j] = arrived[k][slots + j].astype(jnp.float32)

    def subtract(row, term):
        part = pl.ds(pl.multiple_of(row * count, count), count)
        total[part, :] -= term

    for g in range(doms):
        for j in range(slots):
            subtract(send[0, 0, 0, g, j], back[g * slots + j])
    for p in range(0, turned.shape[0], 2):
        first, second = (foreign[peer[0, 0, 0, q] * slots + slot[0, 0, 0, q]] for q in (p, p + 1))
        for q, term in zip((p, p + 1), pair_dot(first, second, turned[p : p + 2])):
            subtract(own[0, 0, 0, q], term)


def finish(total, modes, stiff, halo, out):
    rows = stiff.shape[1]
    count = total.shape[0] // rows
    for m in range(count):
        out[m * rows : (m + 1) * rows, :] = total[pl.ds(m, rows, stride=count), :]
    for side, row in enumerate((0, rows - 1)):
        here = modes[pl.ds(row, count, stride=rows), :]
        near = whole(halo[side, 0], halo[side, 1])
        weight = 0.5 * (stiff[0, row : row + 1, :] + whole(halo[side, 2, 0:1], halo[side, 2, 1:2]))
        out[pl.ds(row, count, stride=rows), :] = total[row * count : (row + 1) * count, :] + weight * (here - near)


def exchange(doms):
    if doms == 4:
        return [3, 1, 2, 0]
    return list(range(doms))


def shards(doms, subs, modes_in, stiffness, coupling, pair_own, pair_peer, pair_slot, send_rows):
    _, count, rows, cells = modes_in.shape
    slots, pairs = send_rows.shape[-1], coupling.shape[3]
    flat = modes_in.reshape(count * rows, cells)
    inputs = (pair_own, pair_peer, pair_slot, send_rows, flat, stiffness, coupling)
    *inputs, coupling = [pltpu.with_memory_space_constraint(a, pltpu.HBM) for a in inputs]
    params = pltpu.CompilerParams(vmem_limit_bytes=32 * 1024 * 1024)
    like = jax.ShapeDtypeStruct
    indices = inputs[:4]
    *outgoing, column, blocks, modes, stiff, own, peer, slot, send = pl.pallas_call(
        functools.partial(before, doms, slots, rows),
        out_shape=[like((2 * slots + PIECES * has_halo(k), count, cells), jnp.bfloat16) for k in range(doms)]
        + [
            like((2, rows, cells), jnp.float32),
            like((pairs, cells, cells), jnp.bfloat16),
            like(flat.shape, jnp.float32),
            like(stiffness.shape, jnp.float32),
        ]
        + [pltpu.SMEM(a.shape, a.dtype) for a in indices],
        in_specs=[HBM] * 7,
        out_specs=[VMEM] * (doms + 4) + [SMEM] * 4,
        scratch_shapes=[
            pltpu.VMEM((rows, count, cells), jnp.bfloat16),
            pltpu.VMEM((doms * slots, count, cells), jnp.float32),
            pltpu.SemaphoreType.DMA((len(inputs),)),
            pltpu.SemaphoreType.DMA((2,)),
        ],
        compiler_params=params,
        name="before",
    )(*inputs, coupling)
    indices = [pltpu.with_memory_space_constraint(a, pltpu.SMEM) for a in (own, peer, slot, send)]
    arrived = {}
    for k in exchange(doms):
        route = [(2 * d + h, 2 * (d ^ k) + 1 - h) for d in range(doms) for h in range(2)]
        arrived[k] = lax.ppermute(outgoing[k], ("dom", "mesh"), route)
    if subs == 1:
        columns = []
    elif subs == 2:
        columns = [lax.ppermute(column, "sub", [(0, 1), (1, 0)])]
    else:
        columns = [
            lax.ppermute(column, "sub", [(i, i + 1) for i in range(subs - 1)]),
            lax.ppermute(column, "sub", [(i + 1, i) for i in range(subs - 1)]),
        ]
    cost = pl.CostEstimate(flops=0, bytes_accessed=8 << 20, transcendentals=0)
    turned = pl.pallas_call(
        turn,
        out_shape=like(blocks.shape, blocks.dtype),
        in_specs=[VMEM],
        out_specs=VMEM,
        compiler_params=params,
        cost_estimate=cost,
        name="turn",
    )(blocks)
    partial = pl.pallas_call(
        functools.partial(stencil, subs),
        out_shape=like(flat.shape, jnp.float32),
        in_specs=[VMEM] * (2 + len(columns)),
        out_specs=VMEM,
        compiler_params=params,
        name="stencil",
    )(modes, stiff, *columns)
    halo = pl.pallas_call(
        functools.partial(pick, doms, slots),
        out_shape=like((2, PIECES, count, cells), jnp.bfloat16),
        in_specs=[VMEM] * sum(map(has_halo, range(doms))) + [ANY] * 2,
        out_specs=VMEM,
        compiler_params=params,
        name="pick",
    )(*(arrived[k] for k in exchange(doms) if has_halo(k)), turned, partial)
    halo = lax.ppermute(halo, "mesh", [(0, 1), (1, 0)])
    total = pl.pallas_call(
        functools.partial(couple, doms, slots),
        out_shape=like(partial.shape, partial.dtype),
        in_specs=[SMEM] * 4 + [VMEM] * (2 + doms),
        out_specs=VMEM,
        scratch_shapes=[
            pltpu.VMEM((doms * slots, count, cells), jnp.bfloat16),
            pltpu.VMEM((doms * slots, count, cells), jnp.float32),
        ],
        input_output_aliases={5 + doms: 0},
        compiler_params=params,
        cost_estimate=cost,
        name="couple",
    )(*indices, turned, *(arrived[k] for k in exchange(doms)), partial)
    out = pl.pallas_call(
        finish,
        out_shape=like(flat.shape, jnp.float32),
        in_specs=[VMEM] * 4,
        out_specs=VMEM,
        compiler_params=params,
        name="finish",
    )(total, modes, stiff, halo)
    return out.reshape(modes_in.shape)


def solution(mesh):
    return jax.shard_map(
        functools.partial(shards, mesh.shape["dom"], mesh.shape["sub"]),
        mesh=mesh,
        in_specs=(
            P("mesh", "copies", "dom", "sub"),
            P(("copies", "mesh"), "dom", "sub"),
            P("mesh", "dom", "sub", None, None, None),
            P("mesh", "dom", "sub", None),
            P("mesh", "dom", "sub", None),
            P("mesh", "dom", "sub", None),
            P("mesh", "dom", "sub", None, None),
        ),
        out_specs=P("mesh", "copies", "dom", "sub"),
        check_vma=False,
    )
```

```python
import functools

import jax
import jax.numpy as jnp
from jax import lax
from jax.experimental import pallas as pl
from jax.experimental.pallas import tpu as pltpu
from jax.sharding import PartitionSpec as P

helm_shift = 1.0
PIECES = 3
SMEM = pl.BlockSpec(memory_space=pltpu.SMEM)
VMEM = pl.BlockSpec(memory_space=pltpu.VMEM)
ANY = pl.BlockSpec(memory_space=pl.ANY)
HBM = pl.BlockSpec(memory_space=pltpu.HBM)


def has_halo(k):
    return k > 0 and k & (k + 1) == 0


def pieces(x):
    high = x.astype(jnp.bfloat16)
    return high, (x - high.astype(jnp.float32)).astype(jnp.bfloat16)


def whole(high, low):
    return high.astype(jnp.float32) + low.astype(jnp.float32)


def pair_dot(a, b, blocks):
    none = jnp.zeros_like(a)
    rows = jnp.concatenate([jnp.concatenate([a, none], 1), jnp.concatenate([none, b], 1)], 0)
    both = jnp.dot(rows, blocks.reshape(2 * blocks.shape[1], -1), preferred_element_type=jnp.float32)
    return both[: a.shape[0]], both[a.shape[0] :]


def load(sources, targets, sems, priority=0):
    copies = [pltpu.make_async_copy(a, b, sems.at[i]) for i, (a, b) in enumerate(zip(sources, targets))]
    for copy in copies:
        copy.start(priority=priority)
    return copies


def before(doms, slots, rows, own_in, peer_in, slot_in, send_in, modes_in, stiff_in, coupling, *refs):
    outs, (column, blocks, modes, stiff) = refs[:doms], refs[doms : doms + 4]
    own, peer, slot, send, tiles, sums, sems, block_sems = refs[doms + 4 :]
    sources = (own_in, peer_in, slot_in, send_in, modes_in, stiff_in)
    copies = load(sources, (own, peer, slot, send, modes, stiff), sems)
    half = blocks.shape[0] // 2
    parts = [pl.ds(0, half), pl.ds(half, half)]
    block_copies = load([coupling.at[0, 0, 0, part] for part in parts], [blocks.at[part] for part in parts], block_sems, 1)
    d = lax.axis_index("dom")
    count, cells = tiles.shape[1:]
    sums[...] = jnp.zeros_like(sums)
    for copy in copies:
        copy.wait()
    for r in range(rows):
        tiles[r] = modes[pl.ds(r, count, stride=rows), :].astype(jnp.bfloat16)

    for k in filter(has_halo, range(doms)):
        row = jnp.where(d ^ k > d, rows - 1, 0)
        edge = modes[pl.ds(row, count, stride=rows), :]
        for i, piece in enumerate(pieces(edge)):
            outs[k][2 * slots + i] = piece
        edge = jnp.broadcast_to(stiff[0, pl.ds(row, 1), :], edge.shape)
        line = lax.broadcasted_iota(jnp.int32, edge.shape, 0)
        high, low = (p.astype(jnp.float32) for p in pieces(edge))
        outs[k][2 * slots + 2] = jnp.where(line == 0, high, low).astype(jnp.bfloat16)
    for k in range(doms):
        for j in range(slots):
            outs[k][j] = tiles[send[0, 0, 0, d ^ k, j]]
    lane = lax.broadcasted_iota(jnp.int32, (rows, cells), 1)
    ends = [jnp.zeros((rows, cells), jnp.float32)] * 2
    for m in range(count + 1):
        here = stiff[0] if m == count else modes[m * rows : (m + 1) * rows, :]
        ends = [jnp.where(lane == m, end, packed) for end, packed in zip((here[:, :1], here[:, -1:]), ends)]
    for side in range(2):
        column[side] = ends[side]
    for c, copy in enumerate(block_copies):
        copy.wait()
        for p in range(c * half, (c + 1) * half, 2):
            terms = pair_dot(tiles[own[0, 0, 0, p]], tiles[own[0, 0, 0, p + 1]], blocks[p : p + 2])
            for q, term in zip((p, p + 1), terms):
                sums[peer[0, 0, 0, q] * slots + slot[0, 0, 0, q]] += term
    for k in range(doms):
        for j in range(slots):
            outs[k][slots + j] = sums[(d ^ k) * slots + j].astype(jnp.bfloat16)


def turn(blocks, turned):
    for p in range(blocks.shape[0]):
        turned[p] = blocks[p].T


def stencil(subs, modes, stiff, *refs):
    columns, total = refs[:-1], refs[-1]
    rows, cells = stiff.shape[1:]
    count = modes.shape[0] // rows
    shift = helm_shift * lax.axis_index("mesh").astype(jnp.float32)
    lane = lax.broadcasted_iota(jnp.int32, (rows, cells), 1)
    line = lax.broadcasted_iota(jnp.int32, (rows, cells), 0)
    first_lane, last_lane = lane == 0, lane == cells - 1
    first_line, last_line = line == 0, line == rows - 1
    s = lax.axis_index("sub")
    if subs == 1:
        left = right = jnp.zeros(lane.shape, jnp.float32)
    elif subs == 2:
        left, right = jnp.where(s == 1, columns[0][1], 0.0), jnp.where(s == 0, columns[0][0], 0.0)
    else:
        left, right = columns[0][1], columns[1][0]

    def near_by(here, m):
        return (
            jnp.where(first_line, here, pltpu.roll(here, 1, 0)),
            jnp.where(last_line, here, pltpu.roll(here, rows - 1, 0)),
            jnp.where(first_lane, left[:, m : m + 1], pltpu.roll(here, 1, 1)),
            jnp.where(last_lane, right[:, m : m + 1], pltpu.roll(here, cells - 1, 1)),
        )

    weights = [0.5 * (stiff[0] + near) for near in near_by(stiff[0], count)]
    for m in range(count):
        here = modes[m * rows : (m + 1) * rows, :]
        result = -shift * here
        for weight, near in zip(weights, near_by(here, m)):
            result = result + weight * (here - near)
        total[pl.ds(m, rows, stride=count), :] = result


def pick(doms, slots, *refs):
    arrived, halo = dict(zip(filter(has_halo, exchange(doms)), refs)), refs[-1]
    d = lax.axis_index("dom")
    halo[...] = jnp.zeros_like(halo)
    for k, ref in arrived.items():
        for side, step in enumerate((-1, 1)):

            @pl.when(d ^ k == d + step)
            def _():
                halo[side] = ref[2 * slots : 2 * slots + PIECES]


def couple(doms, slots, own, peer, slot, send, turned, *refs):
    arrived, (_, total, out, foreign, back) = dict(zip(exchange(doms), refs)), refs[doms:]
    count = foreign.shape[1]
    rows = total.shape[0] // count
    d = lax.axis_index("dom")
    for k in range(doms):
        for j in range(slots):
            foreign[(d ^ k) * slots + j] = arrived[k][j]
            back[(d ^ k) * slots + j] = arrived[k][slots + j].astype(jnp.float32)

    def subtract(row, term):
        part = pl.ds(pl.multiple_of(row * count, count), count)
        total[part, :] -= term

    for g in range(doms):
        for j in range(slots):
            subtract(send[0, 0, 0, g, j], back[g * slots + j])
    for p in range(0, turned.shape[0], 2):
        first, second = (foreign[peer[0, 0, 0, q] * slots + slot[0, 0, 0, q]] for q in (p, p + 1))
        for q, term in zip((p, p + 1), pair_dot(first, second, turned[p : p + 2])):
            subtract(own[0, 0, 0, q], term)
    for m in range(count):
        out[m * rows : (m + 1) * rows, :] = total[pl.ds(m, rows, stride=count), :]


def finish(modes, stiff, halo, _, result, out, sem):
    rows = stiff.shape[1]
    count = modes.shape[0] // rows
    for side, row in enumerate((0, rows - 1)):
        line = pl.ds(row, count, stride=rows)
        here = modes[line, :]
        near = whole(halo[side, 0], halo[side, 1])
        weight = 0.5 * (stiff[0, row : row + 1, :] + whole(halo[side, 2, 0:1], halo[side, 2, 1:2]))
        result[line, :] += weight * (here - near)
    copy = pltpu.make_async_copy(result, out, sem)
    copy.start()
    copy.wait()


def exchange(doms):
    if doms == 4:
        return [3, 1, 2, 0]
    return list(range(doms))


def shards(doms, subs, modes_in, stiffness, coupling, pair_own, pair_peer, pair_slot, send_rows):
    _, count, rows, cells = modes_in.shape
    slots, pairs = send_rows.shape[-1], coupling.shape[3]
    flat = modes_in.reshape(count * rows, cells)
    inputs = (pair_own, pair_peer, pair_slot, send_rows, flat, stiffness, coupling)
    *inputs, coupling = [pltpu.with_memory_space_constraint(a, pltpu.HBM) for a in inputs]
    params = pltpu.CompilerParams(vmem_limit_bytes=32 * 1024 * 1024)
    like = jax.ShapeDtypeStruct
    indices = inputs[:4]
    *outgoing, column, blocks, modes, stiff, own, peer, slot, send = pl.pallas_call(
        functools.partial(before, doms, slots, rows),
        out_shape=[like((2 * slots + PIECES * has_halo(k), count, cells), jnp.bfloat16) for k in range(doms)]
        + [
            like((2, rows, cells), jnp.float32),
            like((pairs, cells, cells), jnp.bfloat16),
            like(flat.shape, jnp.float32),
            like(stiffness.shape, jnp.float32),
        ]
        + [pltpu.SMEM(a.shape, a.dtype) for a in indices],
        in_specs=[HBM] * 7,
        out_specs=[VMEM] * (doms + 4) + [SMEM] * 4,
        scratch_shapes=[
            pltpu.VMEM((rows, count, cells), jnp.bfloat16),
            pltpu.VMEM((doms * slots, count, cells), jnp.float32),
            pltpu.SemaphoreType.DMA((len(inputs),)),
            pltpu.SemaphoreType.DMA((2,)),
        ],
        compiler_params=params,
        name="before",
    )(*inputs, coupling)
    indices = [pltpu.with_memory_space_constraint(a, pltpu.SMEM) for a in (own, peer, slot, send)]
    arrived = {}
    for k in exchange(doms):
        route = [(2 * d + h, 2 * (d ^ k) + 1 - h) for d in range(doms) for h in range(2)]
        arrived[k] = lax.ppermute(outgoing[k], ("dom", "mesh"), route)
    if subs == 1:
        columns = []
    elif subs == 2:
        columns = [lax.ppermute(column, "sub", [(0, 1), (1, 0)])]
    else:
        columns = [
            lax.ppermute(column, "sub", [(i, i + 1) for i in range(subs - 1)]),
            lax.ppermute(column, "sub", [(i + 1, i) for i in range(subs - 1)]),
        ]
    cost = pl.CostEstimate(flops=0, bytes_accessed=8 << 20, transcendentals=0)
    turned = pl.pallas_call(
        turn,
        out_shape=like(blocks.shape, blocks.dtype),
        in_specs=[VMEM],
        out_specs=VMEM,
        compiler_params=params,
        cost_estimate=cost,
        name="turn",
    )(blocks)
    partial = pl.pallas_call(
        functools.partial(stencil, subs),
        out_shape=like(flat.shape, jnp.float32),
        in_specs=[VMEM] * (2 + len(columns)),
        out_specs=VMEM,
        compiler_params=params,
        name="stencil",
    )(modes, stiff, *columns)
    halo = pl.pallas_call(
        functools.partial(pick, doms, slots),
        out_shape=like((2, PIECES, count, cells), jnp.bfloat16),
        in_specs=[VMEM] * sum(map(has_halo, range(doms))) + [ANY] * 2,
        out_specs=VMEM,
        compiler_params=params,
        name="pick",
    )(*(arrived[k] for k in exchange(doms) if has_halo(k)), turned, partial)
    halo = lax.ppermute(halo, "mesh", [(0, 1), (1, 0)])
    _, result = pl.pallas_call(
        functools.partial(couple, doms, slots),
        out_shape=[like(partial.shape, partial.dtype)] * 2,
        in_specs=[SMEM] * 4 + [VMEM] * (2 + doms),
        out_specs=[VMEM] * 2,
        scratch_shapes=[
            pltpu.VMEM((doms * slots, count, cells), jnp.bfloat16),
            pltpu.VMEM((doms * slots, count, cells), jnp.float32),
        ],
        input_output_aliases={5 + doms: 0},
        compiler_params=params,
        cost_estimate=cost,
        name="couple",
    )(*indices, turned, *(arrived[k] for k in exchange(doms)), partial)
    _, out = pl.pallas_call(
        finish,
        out_shape=[like(flat.shape, jnp.float32)] * 2,
        in_specs=[VMEM] * 4,
        out_specs=[VMEM, HBM],
        scratch_shapes=[pltpu.SemaphoreType.DMA],
        input_output_aliases={3: 0},
        compiler_params=params,
        name="finish",
    )(modes, stiff, halo, result)
    return out.reshape(modes_in.shape)


def solution(mesh):
    return jax.shard_map(
        functools.partial(shards, mesh.shape["dom"], mesh.shape["sub"]),
        mesh=mesh,
        in_specs=(
            P("mesh", "copies", "dom", "sub"),
            P(("copies", "mesh"), "dom", "sub"),
            P("mesh", "dom", "sub", None, None, None),
            P("mesh", "dom", "sub", None),
            P("mesh", "dom", "sub", None),
            P("mesh", "dom", "sub", None),
            P("mesh", "dom", "sub", None, None),
        ),
        out_specs=P("mesh", "copies", "dom", "sub"),
        check_vma=False,
    )
```

```python
import functools

import jax
import jax.numpy as jnp
from jax import lax
from jax.experimental import pallas as pl
from jax.experimental.pallas import tpu as pltpu
from jax.sharding import PartitionSpec as P

helm_shift = 1.0
PIECES = 3
SMEM = pl.BlockSpec(memory_space=pltpu.SMEM)
VMEM = pl.BlockSpec(memory_space=pltpu.VMEM)
ANY = pl.BlockSpec(memory_space=pl.ANY)
HBM = pl.BlockSpec(memory_space=pltpu.HBM)


def has_halo(k):
    return k > 0 and k & (k + 1) == 0


def pieces(x):
    high = x.astype(jnp.bfloat16)
    return high, (x - high.astype(jnp.float32)).astype(jnp.bfloat16)


def whole(high, low):
    return high.astype(jnp.float32) + low.astype(jnp.float32)


def pair_dot(a, b, blocks):
    none = jnp.zeros_like(a)
    rows = jnp.concatenate([jnp.concatenate([a, none], 1), jnp.concatenate([none, b], 1)], 0)
    both = jnp.dot(rows, blocks.reshape(2 * blocks.shape[1], -1), preferred_element_type=jnp.float32)
    return both[: a.shape[0]], both[a.shape[0] :]


def load(sources, targets, sems, priority=0):
    copies = [pltpu.make_async_copy(a, b, sems.at[i]) for i, (a, b) in enumerate(zip(sources, targets))]
    for copy in copies:
        copy.start(priority=priority)
    return copies


def before(doms, slots, rows, own_in, peer_in, slot_in, send_in, modes_in, stiff_in, coupling, *refs):
    outs, (column, blocks, modes, stiff) = refs[:doms], refs[doms : doms + 4]
    own, peer, slot, send, tiles, sums, sems, block_sems = refs[doms + 4 :]
    sources = (own_in, peer_in, slot_in, send_in, modes_in, stiff_in)
    copies = load(sources, (own, peer, slot, send, modes, stiff), sems)
    half = blocks.shape[0] // 2
    parts = [pl.ds(0, half), pl.ds(half, half)]
    block_copies = load([coupling.at[0, 0, 0, part] for part in parts], [blocks.at[part] for part in parts], block_sems, 1)
    d = lax.axis_index("dom")
    count, cells = tiles.shape[1:]
    sums[...] = jnp.zeros_like(sums)
    for copy in copies:
        copy.wait()
    for r in range(rows):
        tiles[r] = modes[pl.ds(r, count, stride=rows), :].astype(jnp.bfloat16)

    for k in filter(has_halo, range(doms)):
        last = d ^ k > d
        edge = jnp.where(last, modes[pl.ds(rows - 1, count, stride=rows), :], modes[pl.ds(0, count, stride=rows), :])
        for i, piece in enumerate(pieces(edge)):
            outs[k][2 * slots + i] = piece
        edge = jnp.broadcast_to(jnp.where(last, stiff[0, rows - 1 : rows, :], stiff[0, 0:1, :]), edge.shape)
        line = lax.broadcasted_iota(jnp.int32, edge.shape, 0)
        high, low = (p.astype(jnp.float32) for p in pieces(edge))
        outs[k][2 * slots + 2] = jnp.where(line == 0, high, low).astype(jnp.bfloat16)
    for k in range(doms):
        for j in range(slots):
            outs[k][j] = tiles[send[0, 0, 0, d ^ k, j]]
    lane = lax.broadcasted_iota(jnp.int32, (rows, cells), 1)
    ends = [jnp.zeros((rows, cells), jnp.float32)] * 2
    for m in range(count + 1):
        here = stiff[0] if m == count else modes[m * rows : (m + 1) * rows, :]
        ends = [jnp.where(lane == m, end, packed) for end, packed in zip((here[:, :1], here[:, -1:]), ends)]
    for side in range(2):
        column[side] = ends[side]
    for c, copy in enumerate(block_copies):
        copy.wait()
        for p in range(c * half, (c + 1) * half, 2):
            terms = pair_dot(tiles[own[0, 0, 0, p]], tiles[own[0, 0, 0, p + 1]], blocks[p : p + 2])
            for q, term in zip((p, p + 1), terms):
                sums[peer[0, 0, 0, q] * slots + slot[0, 0, 0, q]] += term
    for k in range(doms):
        for j in range(slots):
            outs[k][slots + j] = sums[(d ^ k) * slots + j].astype(jnp.bfloat16)


def turn(blocks, turned):
    for p in range(blocks.shape[0]):
        turned[p] = blocks[p].T


def stencil(subs, modes, stiff, *refs):
    columns, total = refs[:-1], refs[-1]
    rows, cells = stiff.shape[1:]
    count = modes.shape[0] // rows
    shift = helm_shift * lax.axis_index("mesh").astype(jnp.float32)
    lane = lax.broadcasted_iota(jnp.int32, (rows, cells), 1)
    line = lax.broadcasted_iota(jnp.int32, (rows, cells), 0)
    first_lane, last_lane = lane == 0, lane == cells - 1
    first_line, last_line = line == 0, line == rows - 1
    s = lax.axis_index("sub")
    if subs == 1:
        left = right = jnp.zeros(lane.shape, jnp.float32)
    elif subs == 2:
        left, right = jnp.where(s == 1, columns[0][1], 0.0), jnp.where(s == 0, columns[0][0], 0.0)
    else:
        left, right = columns[0][1], columns[1][0]

    def near_by(here, m):
        return (
            jnp.where(first_line, here, pltpu.roll(here, 1, 0)),
            jnp.where(last_line, here, pltpu.roll(here, rows - 1, 0)),
            jnp.where(first_lane, left[:, m : m + 1], pltpu.roll(here, 1, 1)),
            jnp.where(last_lane, right[:, m : m + 1], pltpu.roll(here, cells - 1, 1)),
        )

    weights = [0.5 * (stiff[0] + near) for near in near_by(stiff[0], count)]
    for m in range(count):
        here = modes[m * rows : (m + 1) * rows, :]
        result = -shift * here
        for weight, near in zip(weights, near_by(here, m)):
            result = result + weight * (here - near)
        total[pl.ds(m, rows, stride=count), :] = result


def pick(doms, slots, *refs):
    arrived, halo = dict(zip(filter(has_halo, exchange(doms)), refs)), refs[-1]
    d = lax.axis_index("dom")
    halo[...] = jnp.zeros_like(halo)
    for k, ref in arrived.items():
        for side, step in enumerate((-1, 1)):

            @pl.when(d ^ k == d + step)
            def _():
                halo[side] = ref[2 * slots : 2 * slots + PIECES]


def couple(doms, slots, own, peer, slot, send, turned, *refs):
    arrived, (_, total, out, foreign, back) = dict(zip(exchange(doms), refs)), refs[doms:]
    count = foreign.shape[1]
    rows = total.shape[0] // count
    d = lax.axis_index("dom")
    for k in range(doms):
        for j in range(slots):
            foreign[(d ^ k) * slots + j] = arrived[k][j]
            back[(d ^ k) * slots + j] = arrived[k][slots + j].astype(jnp.float32)

    def subtract(row, term):
        part = pl.ds(pl.multiple_of(row * count, count), count)
        total[part, :] -= term

    for g in range(doms):
        for j in range(slots):
            subtract(send[0, 0, 0, g, j], back[g * slots + j])
    for p in range(0, turned.shape[0], 2):
        first, second = (foreign[peer[0, 0, 0, q] * slots + slot[0, 0, 0, q]] for q in (p, p + 1))
        for q, term in zip((p, p + 1), pair_dot(first, second, turned[p : p + 2])):
            subtract(own[0, 0, 0, q], term)
    for m in range(count):
        out[m * rows : (m + 1) * rows, :] = total[pl.ds(m, rows, stride=count), :]


def finish(modes, stiff, halo, _, result, out, sem):
    rows = stiff.shape[1]
    count = modes.shape[0] // rows
    for side, row in enumerate((0, rows - 1)):
        line = pl.ds(row, count, stride=rows)
        here = modes[line, :]
        near = whole(halo[side, 0], halo[side, 1])
        weight = 0.5 * (stiff[0, row : row + 1, :] + whole(halo[side, 2, 0:1], halo[side, 2, 1:2]))
        result[line, :] += weight * (here - near)
    copy = pltpu.make_async_copy(result, out, sem)
    copy.start()
    copy.wait()


def exchange(doms):
    if doms == 4:
        return [3, 1, 2, 0]
    return list(range(doms))


def shards(doms, subs, modes_in, stiffness, coupling, pair_own, pair_peer, pair_slot, send_rows):
    _, count, rows, cells = modes_in.shape
    slots, pairs = send_rows.shape[-1], coupling.shape[3]
    flat = modes_in.reshape(count * rows, cells)
    inputs = (pair_own, pair_peer, pair_slot, send_rows, flat, stiffness, coupling)
    *inputs, coupling = [pltpu.with_memory_space_constraint(a, pltpu.HBM) for a in inputs]
    params = pltpu.CompilerParams(vmem_limit_bytes=32 * 1024 * 1024)
    like = jax.ShapeDtypeStruct
    indices = inputs[:4]
    *outgoing, column, blocks, modes, stiff, own, peer, slot, send = pl.pallas_call(
        functools.partial(before, doms, slots, rows),
        out_shape=[like((2 * slots + PIECES * has_halo(k), count, cells), jnp.bfloat16) for k in range(doms)]
        + [
            like((2, rows, cells), jnp.float32),
            like((pairs, cells, cells), jnp.bfloat16),
            like(flat.shape, jnp.float32),
            like(stiffness.shape, jnp.float32),
        ]
        + [pltpu.SMEM(a.shape, a.dtype) for a in indices],
        in_specs=[HBM] * 7,
        out_specs=[VMEM] * (doms + 4) + [SMEM] * 4,
        scratch_shapes=[
            pltpu.VMEM((rows, count, cells), jnp.bfloat16),
            pltpu.VMEM((doms * slots, count, cells), jnp.float32),
            pltpu.SemaphoreType.DMA((len(inputs),)),
            pltpu.SemaphoreType.DMA((2,)),
        ],
        compiler_params=params,
        name="before",
    )(*inputs, coupling)
    indices = [pltpu.with_memory_space_constraint(a, pltpu.SMEM) for a in (own, peer, slot, send)]
    arrived = {}
    for k in exchange(doms):
        route = [(2 * d + h, 2 * (d ^ k) + 1 - h) for d in range(doms) for h in range(2)]
        arrived[k] = lax.ppermute(outgoing[k], ("dom", "mesh"), route)
    if subs == 1:
        columns = []
    elif subs == 2:
        columns = [lax.ppermute(column, "sub", [(0, 1), (1, 0)])]
    else:
        columns = [
            lax.ppermute(column, "sub", [(i, i + 1) for i in range(subs - 1)]),
            lax.ppermute(column, "sub", [(i + 1, i) for i in range(subs - 1)]),
        ]
    cost = pl.CostEstimate(flops=0, bytes_accessed=8 << 20, transcendentals=0)
    turned = pl.pallas_call(
        turn,
        out_shape=like(blocks.shape, blocks.dtype),
        in_specs=[VMEM],
        out_specs=VMEM,
        compiler_params=params,
        cost_estimate=cost,
        name="turn",
    )(blocks)
    partial = pl.pallas_call(
        functools.partial(stencil, subs),
        out_shape=like(flat.shape, jnp.float32),
        in_specs=[VMEM] * (2 + len(columns)),
        out_specs=VMEM,
        compiler_params=params,
        name="stencil",
    )(modes, stiff, *columns)
    halo = pl.pallas_call(
        functools.partial(pick, doms, slots),
        out_shape=like((2, PIECES, count, cells), jnp.bfloat16),
        in_specs=[VMEM] * sum(map(has_halo, range(doms))) + [ANY] * 2,
        out_specs=VMEM,
        compiler_params=params,
        name="pick",
    )(*(arrived[k] for k in exchange(doms) if has_halo(k)), turned, partial)
    halo = lax.ppermute(halo, "mesh", [(0, 1), (1, 0)])
    _, result = pl.pallas_call(
        functools.partial(couple, doms, slots),
        out_shape=[like(partial.shape, partial.dtype)] * 2,
        in_specs=[SMEM] * 4 + [VMEM] * (2 + doms),
        out_specs=[VMEM] * 2,
        scratch_shapes=[
            pltpu.VMEM((doms * slots, count, cells), jnp.bfloat16),
            pltpu.VMEM((doms * slots, count, cells), jnp.float32),
        ],
        input_output_aliases={5 + doms: 0},
        compiler_params=params,
        cost_estimate=cost,
        name="couple",
    )(*indices, turned, *(arrived[k] for k in exchange(doms)), partial)
    _, out = pl.pallas_call(
        finish,
        out_shape=[like(flat.shape, jnp.float32)] * 2,
        in_specs=[VMEM] * 4,
        out_specs=[VMEM, HBM],
        scratch_shapes=[pltpu.SemaphoreType.DMA],
        input_output_aliases={3: 0},
        compiler_params=params,
        name="finish",
    )(modes, stiff, halo, result)
    return out.reshape(modes_in.shape)


def solution(mesh):
    return jax.shard_map(
        functools.partial(shards, mesh.shape["dom"], mesh.shape["sub"]),
        mesh=mesh,
        in_specs=(
            P("mesh", "copies", "dom", "sub"),
            P(("copies", "mesh"), "dom", "sub"),
            P("mesh", "dom", "sub", None, None, None),
            P("mesh", "dom", "sub", None),
            P("mesh", "dom", "sub", None),
            P("mesh", "dom", "sub", None),
            P("mesh", "dom", "sub", None, None),
        ),
        out_specs=P("mesh", "copies", "dom", "sub"),
        check_vma=False,
    )
```

```python
import functools

import jax
import jax.numpy as jnp
from jax import lax
from jax.experimental import pallas as pl
from jax.experimental.pallas import tpu as pltpu
from jax.sharding import PartitionSpec as P

helm_shift = 1.0
PIECES = 3
SMEM = pl.BlockSpec(memory_space=pltpu.SMEM)
VMEM = pl.BlockSpec(memory_space=pltpu.VMEM)
ANY = pl.BlockSpec(memory_space=pl.ANY)
HBM = pl.BlockSpec(memory_space=pltpu.HBM)


def has_halo(k):
    return k > 0 and k & (k + 1) == 0


def pieces(x):
    high = x.astype(jnp.bfloat16)
    return high, (x - high.astype(jnp.float32)).astype(jnp.bfloat16)


def whole(high, low):
    return high.astype(jnp.float32) + low.astype(jnp.float32)


def pair_dot(a, b, blocks):
    none = jnp.zeros_like(a)
    rows = jnp.concatenate([jnp.concatenate([a, none], 1), jnp.concatenate([none, b], 1)], 0)
    both = jnp.dot(rows, blocks.reshape(2 * blocks.shape[1], -1), preferred_element_type=jnp.float32)
    return both[: a.shape[0]], both[a.shape[0] :]


def load(sources, targets, sems, priority=0):
    copies = [pltpu.make_async_copy(a, b, sems.at[i]) for i, (a, b) in enumerate(zip(sources, targets))]
    for copy in copies:
        copy.start(priority=priority)
    return copies


def before(doms, slots, rows, own_in, peer_in, slot_in, send_in, modes_in, stiff_in, coupling, *refs):
    outs, (column, blocks, modes, stiff) = refs[:doms], refs[doms : doms + 4]
    own, peer, slot, send, tiles, sums, sems, block_sems = refs[doms + 4 :]
    sources = (own_in, peer_in, slot_in, send_in, modes_in, stiff_in)
    copies = load(sources, (own, peer, slot, send, modes, stiff), sems)
    half = blocks.shape[0] // 2
    parts = [pl.ds(0, half), pl.ds(half, half)]
    block_copies = load([coupling.at[0, 0, 0, part] for part in parts], [blocks.at[part] for part in parts], block_sems, 1)
    d = lax.axis_index("dom")
    count, cells = tiles.shape[1:]
    sums[...] = jnp.zeros_like(sums)
    for copy in copies:
        copy.wait()
    for r in range(rows):
        tiles[r] = modes[pl.ds(r, count, stride=rows), :].astype(jnp.bfloat16)

    for k in filter(has_halo, range(doms)):
        last = d ^ k > d
        edge = jnp.where(last, modes[pl.ds(rows - 1, count, stride=rows), :], modes[pl.ds(0, count, stride=rows), :])
        for i, piece in enumerate(pieces(edge)):
            outs[k][2 * slots + i] = piece
        edge = jnp.broadcast_to(jnp.where(last, stiff[0, rows - 1 : rows, :], stiff[0, 0:1, :]), edge.shape)
        line = lax.broadcasted_iota(jnp.int32, edge.shape, 0)
        high, low = (p.astype(jnp.float32) for p in pieces(edge))
        outs[k][2 * slots + 2] = jnp.where(line == 0, high, low).astype(jnp.bfloat16)
    for k in range(doms):
        for j in range(slots):
            outs[k][j] = tiles[send[0, 0, 0, d ^ k, j]]
    lane = lax.broadcasted_iota(jnp.int32, (rows, cells), 1)
    ends = [jnp.zeros((rows, cells), jnp.float32)] * 2
    for m in range(count + 1):
        here = stiff[0] if m == count else modes[m * rows : (m + 1) * rows, :]
        ends = [jnp.where(lane == m, end, packed) for end, packed in zip((here[:, :1], here[:, -1:]), ends)]
    for side in range(2):
        column[side] = ends[side]
    for c, copy in enumerate(block_copies):
        copy.wait()
        for p in range(c * half, (c + 1) * half, 2):
            terms = pair_dot(tiles[own[0, 0, 0, p]], tiles[own[0, 0, 0, p + 1]], blocks[p : p + 2])
            for q, term in zip((p, p + 1), terms):
                sums[peer[0, 0, 0, q] * slots + slot[0, 0, 0, q]] += term
    for k in range(doms):
        for j in range(slots):
            outs[k][slots + j] = sums[(d ^ k) * slots + j].astype(jnp.bfloat16)


def turn(blocks, turned):
    for p in range(blocks.shape[0]):
        turned[p] = blocks[p].T


def stencil(subs, modes, stiff, *refs):
    columns, total = refs[:-1], refs[-1]
    rows, cells = stiff.shape[1:]
    count = modes.shape[0] // rows
    shift = helm_shift * lax.axis_index("mesh").astype(jnp.float32)
    lane = lax.broadcasted_iota(jnp.int32, (rows, cells), 1)
    line = lax.broadcasted_iota(jnp.int32, (rows, cells), 0)
    first_lane, last_lane = lane == 0, lane == cells - 1
    first_line, last_line = line == 0, line == rows - 1
    s = lax.axis_index("sub")
    if subs == 1:
        left = right = jnp.zeros(lane.shape, jnp.float32)
    elif subs == 2:
        left, right = jnp.where(s == 1, columns[0][1], 0.0), jnp.where(s == 0, columns[0][0], 0.0)
    else:
        left, right = columns[0][1], columns[1][0]

    def near_by(here, m):
        return (
            jnp.where(first_line, here, pltpu.roll(here, 1, 0)),
            jnp.where(last_line, here, pltpu.roll(here, rows - 1, 0)),
            jnp.where(first_lane, left[:, m : m + 1], pltpu.roll(here, 1, 1)),
            jnp.where(last_lane, right[:, m : m + 1], pltpu.roll(here, cells - 1, 1)),
        )

    weights = [0.5 * (stiff[0] + near) for near in near_by(stiff[0], count)]
    for m in range(count):
        here = modes[m * rows : (m + 1) * rows, :]
        result = -shift * here
        for weight, near in zip(weights, near_by(here, m)):
            result = result + weight * (here - near)
        total[pl.ds(m, rows, stride=count), :] = result


def pick(doms, slots, *refs):
    arrived, halo = dict(zip(filter(has_halo, exchange(doms)), refs)), refs[-1]
    d = lax.axis_index("dom")
    halo[...] = jnp.zeros_like(halo)
    for k, ref in arrived.items():
        for side, step in enumerate((-1, 1)):

            @pl.when(d ^ k == d + step)
            def _():
                halo[side] = ref[2 * slots : 2 * slots + PIECES]


def couple(doms, slots, own, peer, slot, send, turned, *refs):
    arrived, (_, total, foreign, back) = dict(zip(exchange(doms), refs)), refs[doms:]
    count = foreign.shape[1]
    d = lax.axis_index("dom")
    for k in range(doms):
        for j in range(slots):
            foreign[(d ^ k) * slots + j] = arrived[k][j]
            back[(d ^ k) * slots + j] = arrived[k][slots + j].astype(jnp.float32)

    def subtract(row, term):
        part = pl.ds(pl.multiple_of(row * count, count), count)
        total[part, :] -= term

    for g in range(doms):
        for j in range(slots):
            subtract(send[0, 0, 0, g, j], back[g * slots + j])
    for p in range(0, turned.shape[0], 2):
        first, second = (foreign[peer[0, 0, 0, q] * slots + slot[0, 0, 0, q]] for q in (p, p + 1))
        for q, term in zip((p, p + 1), pair_dot(first, second, turned[p : p + 2])):
            subtract(own[0, 0, 0, q], term)


def finish(total, modes, stiff, halo, out):
    rows = stiff.shape[1]
    count = total.shape[0] // rows
    for m in range(count):
        out[m * rows : (m + 1) * rows, :] = total[pl.ds(m, rows, stride=count), :]
    for side, row in enumerate((0, rows - 1)):
        here = modes[pl.ds(row, count, stride=rows), :]
        near = whole(halo[side, 0], halo[side, 1])
        weight = 0.5 * (stiff[0, row : row + 1, :] + whole(halo[side, 2, 0:1], halo[side, 2, 1:2]))
        out[pl.ds(row, count, stride=rows), :] = total[row * count : (row + 1) * count, :] + weight * (here - near)


def exchange(doms):
    if doms == 4:
        return [3, 1, 2, 0]
    return list(range(doms))


def shards(doms, subs, modes_in, stiffness, coupling, pair_own, pair_peer, pair_slot, send_rows):
    _, count, rows, cells = modes_in.shape
    slots, pairs = send_rows.shape[-1], coupling.shape[3]
    flat = modes_in.reshape(count * rows, cells)
    inputs = (pair_own, pair_peer, pair_slot, send_rows, flat, stiffness, coupling)
    *inputs, coupling = [pltpu.with_memory_space_constraint(a, pltpu.HBM) for a in inputs]
    params = pltpu.CompilerParams(vmem_limit_bytes=32 * 1024 * 1024)
    like = jax.ShapeDtypeStruct
    indices = inputs[:4]
    *outgoing, column, blocks, modes, stiff, own, peer, slot, send = pl.pallas_call(
        functools.partial(before, doms, slots, rows),
        out_shape=[like((2 * slots + PIECES * has_halo(k), count, cells), jnp.bfloat16) for k in range(doms)]
        + [
            like((2, rows, cells), jnp.float32),
            like((pairs, cells, cells), jnp.bfloat16),
            like(flat.shape, jnp.float32),
            like(stiffness.shape, jnp.float32),
        ]
        + [pltpu.SMEM(a.shape, a.dtype) for a in indices],
        in_specs=[HBM] * 7,
        out_specs=[VMEM] * (doms + 4) + [SMEM] * 4,
        scratch_shapes=[
            pltpu.VMEM((rows, count, cells), jnp.bfloat16),
            pltpu.VMEM((doms * slots, count, cells), jnp.float32),
            pltpu.SemaphoreType.DMA((len(inputs),)),
            pltpu.SemaphoreType.DMA((2,)),
        ],
        compiler_params=params,
        name="before",
    )(*inputs, coupling)
    indices = [pltpu.with_memory_space_constraint(a, pltpu.SMEM) for a in (own, peer, slot, send)]
    arrived = {}
    for k in exchange(doms):
        route = [(2 * d + h, 2 * (d ^ k) + 1 - h) for d in range(doms) for h in range(2)]
        arrived[k] = lax.ppermute(outgoing[k], ("dom", "mesh"), route)
    if subs == 1:
        columns = []
    elif subs == 2:
        columns = [lax.ppermute(column, "sub", [(0, 1), (1, 0)])]
    else:
        columns = [
            lax.ppermute(column, "sub", [(i, i + 1) for i in range(subs - 1)]),
            lax.ppermute(column, "sub", [(i + 1, i) for i in range(subs - 1)]),
        ]
    cost = pl.CostEstimate(flops=0, bytes_accessed=8 << 20, transcendentals=0)
    turned = pl.pallas_call(
        turn,
        out_shape=like(blocks.shape, blocks.dtype),
        in_specs=[VMEM],
        out_specs=VMEM,
        compiler_params=params,
        cost_estimate=cost,
        name="turn",
    )(blocks)
    partial = pl.pallas_call(
        functools.partial(stencil, subs),
        out_shape=like(flat.shape, jnp.float32),
        in_specs=[VMEM] * (2 + len(columns)),
        out_specs=VMEM,
        compiler_params=params,
        name="stencil",
    )(modes, stiff, *columns)
    halo = pl.pallas_call(
        functools.partial(pick, doms, slots),
        out_shape=like((2, PIECES, count, cells), jnp.bfloat16),
        in_specs=[VMEM] * sum(map(has_halo, range(doms))) + [ANY] * 2,
        out_specs=VMEM,
        compiler_params=params,
        name="pick",
    )(*(arrived[k] for k in exchange(doms) if has_halo(k)), turned, partial)
    halo = lax.ppermute(halo, "mesh", [(0, 1), (1, 0)])
    total = pl.pallas_call(
        functools.partial(couple, doms, slots),
        out_shape=like(partial.shape, partial.dtype),
        in_specs=[SMEM] * 4 + [VMEM] * (2 + doms),
        out_specs=VMEM,
        scratch_shapes=[
            pltpu.VMEM((doms * slots, count, cells), jnp.bfloat16),
            pltpu.VMEM((doms * slots, count, cells), jnp.float32),
        ],
        input_output_aliases={5 + doms: 0},
        compiler_params=params,
        cost_estimate=cost,
        name="couple",
    )(*indices, turned, *(arrived[k] for k in exchange(doms)), partial)
    out = pl.pallas_call(
        finish,
        out_shape=like(flat.shape, jnp.float32),
        in_specs=[VMEM] * 4,
        out_specs=VMEM,
        compiler_params=params,
        name="finish",
    )(total, modes, stiff, halo)
    return out.reshape(modes_in.shape)


def solution(mesh):
    return jax.shard_map(
        functools.partial(shards, mesh.shape["dom"], mesh.shape["sub"]),
        mesh=mesh,
        in_specs=(
            P("mesh", "copies", "dom", "sub"),
            P(("copies", "mesh"), "dom", "sub"),
            P("mesh", "dom", "sub", None, None, None),
            P("mesh", "dom", "sub", None),
            P("mesh", "dom", "sub", None),
            P("mesh", "dom", "sub", None),
            P("mesh", "dom", "sub", None, None),
        ),
        out_specs=P("mesh", "copies", "dom", "sub"),
        check_vma=False,
    )
```

```python
import functools

import jax
import jax.numpy as jnp
from jax import lax
from jax.experimental import pallas as pl
from jax.experimental.pallas import tpu as pltpu
from jax.sharding import PartitionSpec as P

helm_shift = 1.0
PIECES = 3
SMEM = pl.BlockSpec(memory_space=pltpu.SMEM)
VMEM = pl.BlockSpec(memory_space=pltpu.VMEM)
ANY = pl.BlockSpec(memory_space=pl.ANY)
HBM = pl.BlockSpec(memory_space=pltpu.HBM)


def has_halo(k):
    return k > 0 and k & (k + 1) == 0


def pieces(x):
    high = x.astype(jnp.bfloat16)
    return high, (x - high.astype(jnp.float32)).astype(jnp.bfloat16)


def whole(high, low):
    return high.astype(jnp.float32) + low.astype(jnp.float32)


def pair_dot(a, b, blocks):
    none = jnp.zeros_like(a)
    rows = jnp.concatenate([jnp.concatenate([a, none], 1), jnp.concatenate([none, b], 1)], 0)
    both = jnp.dot(rows, blocks.reshape(2 * blocks.shape[1], -1), preferred_element_type=jnp.float32)
    return both[: a.shape[0]], both[a.shape[0] :]


def load(sources, targets, sems, priority=0):
    copies = [pltpu.make_async_copy(a, b, sems.at[i]) for i, (a, b) in enumerate(zip(sources, targets))]
    for copy in copies:
        copy.start(priority=priority)
    return copies


def before(doms, subs, slots, rows, own_in, peer_in, slot_in, send_in, modes_in, stiff_in, coupling, *refs):
    outs, (column, blocks, modes, stiff) = refs[:doms], refs[doms : doms + 4]
    own, peer, slot, send, tiles, sums, sems, block_sems = refs[doms + 4 :]
    sources = (own_in, peer_in, slot_in, send_in, modes_in, stiff_in)
    copies = load(sources, (own, peer, slot, send, modes, stiff), sems)
    half = blocks.shape[0] // 2
    parts = [pl.ds(0, half), pl.ds(half, half)]
    block_copies = load([coupling.at[0, 0, 0, part] for part in parts], [blocks.at[part] for part in parts], block_sems, 1)
    d = lax.axis_index("dom")
    count, cells = tiles.shape[1:]
    sums[...] = jnp.zeros_like(sums)
    for copy in copies:
        copy.wait()
    for r in range(rows):
        tiles[r] = modes[pl.ds(r, count, stride=rows), :].astype(jnp.bfloat16)

    for k in filter(has_halo, range(doms)):
        last = d ^ k > d
        edge = jnp.where(last, modes[pl.ds(rows - 1, count, stride=rows), :], modes[pl.ds(0, count, stride=rows), :])
        for i, piece in enumerate(pieces(edge)):
            outs[k][2 * slots + i] = piece
        edge = jnp.broadcast_to(jnp.where(last, stiff[0, rows - 1 : rows, :], stiff[0, 0:1, :]), edge.shape)
        line = lax.broadcasted_iota(jnp.int32, edge.shape, 0)
        high, low = (p.astype(jnp.float32) for p in pieces(edge))
        outs[k][2 * slots + 2] = jnp.where(line == 0, high, low).astype(jnp.bfloat16)
    for k in range(doms):
        for j in range(slots):
            outs[k][j] = tiles[send[0, 0, 0, d ^ k, j]]
    lane = lax.broadcasted_iota(jnp.int32, (rows, cells), 1)
    ends = [jnp.zeros((rows, cells), jnp.float32)] * 2
    for m in range(count + 1):
        here = stiff[0] if m == count else modes[m * rows : (m + 1) * rows, :]
        ends = [jnp.where(lane == m, end, packed) for end, packed in zip((here[:, :1], here[:, -1:]), ends)]
    if subs == 2:
        column[0] = jnp.where(lax.axis_index("sub") == 0, ends[1], ends[0])
    else:
        for side in range(2):
            column[side] = ends[side]
    for c, copy in enumerate(block_copies):
        copy.wait()
        for p in range(c * half, (c + 1) * half, 2):
            terms = pair_dot(tiles[own[0, 0, 0, p]], tiles[own[0, 0, 0, p + 1]], blocks[p : p + 2])
            for q, term in zip((p, p + 1), terms):
                sums[peer[0, 0, 0, q] * slots + slot[0, 0, 0, q]] += term
    for k in range(doms):
        for j in range(slots):
            outs[k][slots + j] = sums[(d ^ k) * slots + j].astype(jnp.bfloat16)


def turn(blocks, turned):
    for p in range(blocks.shape[0]):
        turned[p] = blocks[p].T


def stencil(subs, modes, stiff, *refs):
    columns, total = refs[:-1], refs[-1]
    rows, cells = stiff.shape[1:]
    count = modes.shape[0] // rows
    shift = helm_shift * lax.axis_index("mesh").astype(jnp.float32)
    lane = lax.broadcasted_iota(jnp.int32, (rows, cells), 1)
    line = lax.broadcasted_iota(jnp.int32, (rows, cells), 0)
    first_lane, last_lane = lane == 0, lane == cells - 1
    first_line, last_line = line == 0, line == rows - 1
    s = lax.axis_index("sub")
    if subs == 1:
        left = right = jnp.zeros(lane.shape, jnp.float32)
    elif subs == 2:
        left, right = jnp.where(s == 1, columns[0][0], 0.0), jnp.where(s == 0, columns[0][0], 0.0)
    else:
        left, right = columns[0][1], columns[1][0]

    def near_by(here, m):
        return (
            jnp.where(first_line, here, pltpu.roll(here, 1, 0)),
            jnp.where(last_line, here, pltpu.roll(here, rows - 1, 0)),
            jnp.where(first_lane, left[:, m : m + 1], pltpu.roll(here, 1, 1)),
            jnp.where(last_lane, right[:, m : m + 1], pltpu.roll(here, cells - 1, 1)),
        )

    weights = [0.5 * (stiff[0] + near) for near in near_by(stiff[0], count)]
    for m in range(count):
        here = modes[m * rows : (m + 1) * rows, :]
        result = -shift * here
        for weight, near in zip(weights, near_by(here, m)):
            result = result + weight * (here - near)
        total[pl.ds(m, rows, stride=count), :] = result


def pick(doms, slots, *refs):
    arrived, halo = dict(zip(filter(has_halo, exchange(doms)), refs)), refs[-1]
    d = lax.axis_index("dom")
    halo[...] = jnp.zeros_like(halo)
    for k, ref in arrived.items():
        for side, step in enumerate((-1, 1)):

            @pl.when(d ^ k == d + step)
            def _():
                halo[side] = ref[2 * slots : 2 * slots + PIECES]


def couple(doms, slots, own, peer, slot, send, turned, *refs):
    arrived, (_, total, foreign, back) = dict(zip(exchange(doms), refs)), refs[doms:]
    count = foreign.shape[1]
    d = lax.axis_index("dom")
    for k in range(doms):
        for j in range(slots):
            foreign[(d ^ k) * slots + j] = arrived[k][j]
            back[(d ^ k) * slots + j] = arrived[k][slots + j].astype(jnp.float32)

    def subtract(row, term):
        part = pl.ds(pl.multiple_of(row * count, count), count)
        total[part, :] -= term

    for g in range(doms):
        for j in range(slots):
            subtract(send[0, 0, 0, g, j], back[g * slots + j])
    for p in range(0, turned.shape[0], 2):
        first, second = (foreign[peer[0, 0, 0, q] * slots + slot[0, 0, 0, q]] for q in (p, p + 1))
        for q, term in zip((p, p + 1), pair_dot(first, second, turned[p : p + 2])):
            subtract(own[0, 0, 0, q], term)


def finish(total, modes, stiff, halo, out):
    rows = stiff.shape[1]
    count = total.shape[0] // rows
    for m in range(count):
        out[m * rows : (m + 1) * rows, :] = total[pl.ds(m, rows, stride=count), :]
    for side, row in enumerate((0, rows - 1)):
        here = modes[pl.ds(row, count, stride=rows), :]
        near = whole(halo[side, 0], halo[side, 1])
        weight = 0.5 * (stiff[0, row : row + 1, :] + whole(halo[side, 2, 0:1], halo[side, 2, 1:2]))
        out[pl.ds(row, count, stride=rows), :] = total[row * count : (row + 1) * count, :] + weight * (here - near)


def exchange(doms):
    if doms == 4:
        return [3, 1, 2, 0]
    return list(range(doms))


def shards(doms, subs, modes_in, stiffness, coupling, pair_own, pair_peer, pair_slot, send_rows):
    _, count, rows, cells = modes_in.shape
    slots, pairs = send_rows.shape[-1], coupling.shape[3]
    flat = modes_in.reshape(count * rows, cells)
    inputs = (pair_own, pair_peer, pair_slot, send_rows, flat, stiffness, coupling)
    *inputs, coupling = [pltpu.with_memory_space_constraint(a, pltpu.HBM) for a in inputs]
    params = pltpu.CompilerParams(vmem_limit_bytes=32 * 1024 * 1024)
    like = jax.ShapeDtypeStruct
    indices = inputs[:4]
    *outgoing, column, blocks, modes, stiff, own, peer, slot, send = pl.pallas_call(
        functools.partial(before, doms, subs, slots, rows),
        out_shape=[like((2 * slots + PIECES * has_halo(k), count, cells), jnp.bfloat16) for k in range(doms)]
        + [
            like((1 if subs == 2 else 2, rows, cells), jnp.float32),
            like((pairs, cells, cells), jnp.bfloat16),
            like(flat.shape, jnp.float32),
            like(stiffness.shape, jnp.float32),
        ]
        + [pltpu.SMEM(a.shape, a.dtype) for a in indices],
        in_specs=[HBM] * 7,
        out_specs=[VMEM] * (doms + 4) + [SMEM] * 4,
        scratch_shapes=[
            pltpu.VMEM((rows, count, cells), jnp.bfloat16),
            pltpu.VMEM((doms * slots, count, cells), jnp.float32),
            pltpu.SemaphoreType.DMA((len(inputs),)),
            pltpu.SemaphoreType.DMA((2,)),
        ],
        compiler_params=params,
        name="before",
    )(*inputs, coupling)
    indices = [pltpu.with_memory_space_constraint(a, pltpu.SMEM) for a in (own, peer, slot, send)]
    arrived = {}
    for k in exchange(doms):
        route = [(2 * d + h, 2 * (d ^ k) + 1 - h) for d in range(doms) for h in range(2)]
        arrived[k] = lax.ppermute(outgoing[k], ("dom", "mesh"), route)
    if subs == 1:
        columns = []
    elif subs == 2:
        columns = [lax.ppermute(column, "sub", [(0, 1), (1, 0)])]
    else:
        columns = [
            lax.ppermute(column, "sub", [(i, i + 1) for i in range(subs - 1)]),
            lax.ppermute(column, "sub", [(i + 1, i) for i in range(subs - 1)]),
        ]
    cost = pl.CostEstimate(flops=0, bytes_accessed=8 << 20, transcendentals=0)
    turned = pl.pallas_call(
        turn,
        out_shape=like(blocks.shape, blocks.dtype),
        in_specs=[VMEM],
        out_specs=VMEM,
        compiler_params=params,
        cost_estimate=cost,
        name="turn",
    )(blocks)
    partial = pl.pallas_call(
        functools.partial(stencil, subs),
        out_shape=like(flat.shape, jnp.float32),
        in_specs=[VMEM] * (2 + len(columns)),
        out_specs=VMEM,
        compiler_params=params,
        name="stencil",
    )(modes, stiff, *columns)
    halo = pl.pallas_call(
        functools.partial(pick, doms, slots),
        out_shape=like((2, PIECES, count, cells), jnp.bfloat16),
        in_specs=[VMEM] * sum(map(has_halo, range(doms))) + [ANY] * 2,
        out_specs=VMEM,
        compiler_params=params,
        name="pick",
    )(*(arrived[k] for k in exchange(doms) if has_halo(k)), turned, partial)
    halo = lax.ppermute(halo, "mesh", [(0, 1), (1, 0)])
    total = pl.pallas_call(
        functools.partial(couple, doms, slots),
        out_shape=like(partial.shape, partial.dtype),
        in_specs=[SMEM] * 4 + [VMEM] * (2 + doms),
        out_specs=VMEM,
        scratch_shapes=[
            pltpu.VMEM((doms * slots, count, cells), jnp.bfloat16),
            pltpu.VMEM((doms * slots, count, cells), jnp.float32),
        ],
        input_output_aliases={5 + doms: 0},
        compiler_params=params,
        cost_estimate=cost,
        name="couple",
    )(*indices, turned, *(arrived[k] for k in exchange(doms)), partial)
    out = pl.pallas_call(
        finish,
        out_shape=like(flat.shape, jnp.float32),
        in_specs=[VMEM] * 4,
        out_specs=VMEM,
        compiler_params=params,
        name="finish",
    )(total, modes, stiff, halo)
    return out.reshape(modes_in.shape)


def solution(mesh):
    return jax.shard_map(
        functools.partial(shards, mesh.shape["dom"], mesh.shape["sub"]),
        mesh=mesh,
        in_specs=(
            P("mesh", "copies", "dom", "sub"),
            P(("copies", "mesh"), "dom", "sub"),
            P("mesh", "dom", "sub", None, None, None),
            P("mesh", "dom", "sub", None),
            P("mesh", "dom", "sub", None),
            P("mesh", "dom", "sub", None),
            P("mesh", "dom", "sub", None, None),
        ),
        out_specs=P("mesh", "copies", "dom", "sub"),
        check_vma=False,
    )
```

```python
import functools

import jax
import jax.numpy as jnp
from jax import lax
from jax.experimental import pallas as pl
from jax.experimental.pallas import tpu as pltpu
from jax.sharding import PartitionSpec as P

helm_shift = 1.0
PIECES = 3
SMEM = pl.BlockSpec(memory_space=pltpu.SMEM)
VMEM = pl.BlockSpec(memory_space=pltpu.VMEM)
ANY = pl.BlockSpec(memory_space=pl.ANY)
HBM = pl.BlockSpec(memory_space=pltpu.HBM)


def has_halo(k):
    return k > 0 and k & (k + 1) == 0


def pieces(x):
    high = x.astype(jnp.bfloat16)
    return high, (x - high.astype(jnp.float32)).astype(jnp.bfloat16)


def whole(high, low):
    return high.astype(jnp.float32) + low.astype(jnp.float32)


def pair_dot(a, b, blocks):
    none = jnp.zeros_like(a)
    rows = jnp.concatenate([jnp.concatenate([a, none], 1), jnp.concatenate([none, b], 1)], 0)
    both = jnp.dot(rows, blocks.reshape(2 * blocks.shape[1], -1), preferred_element_type=jnp.float32)
    return both[: a.shape[0]], both[a.shape[0] :]


def load(sources, targets, sems, priority=0):
    copies = [pltpu.make_async_copy(a, b, sems.at[i]) for i, (a, b) in enumerate(zip(sources, targets))]
    for copy in copies:
        copy.start(priority=priority)
    return copies


def before(doms, subs, slots, rows, own_in, peer_in, slot_in, send_in, modes_in, stiff_in, coupling, *refs):
    outs, (column, blocks, modes, stiff) = refs[:doms], refs[doms : doms + 4]
    own, peer, slot, send, tiles, sums, sems, block_sems = refs[doms + 4 :]
    sources = (own_in, peer_in, slot_in, send_in, modes_in, stiff_in)
    copies = load(sources, (own, peer, slot, send, modes, stiff), sems)
    half = blocks.shape[0] // 2
    parts = [pl.ds(0, half), pl.ds(half, half)]
    block_copies = load([coupling.at[0, 0, 0, part] for part in parts], [blocks.at[part] for part in parts], block_sems, 1)
    d = lax.axis_index("dom")
    count, cells = tiles.shape[1:]
    sums[...] = jnp.zeros_like(sums)
    for copy in copies:
        copy.wait()
    for r in range(rows):
        tiles[r] = modes[pl.ds(r, count, stride=rows), :].astype(jnp.bfloat16)

    for k in filter(has_halo, range(doms)):
        last = d ^ k > d
        edge = jnp.where(last, modes[pl.ds(rows - 1, count, stride=rows), :], modes[pl.ds(0, count, stride=rows), :])
        for i, piece in enumerate(pieces(edge)):
            outs[k][2 * slots + i] = piece
        edge = jnp.broadcast_to(jnp.where(last, stiff[0, rows - 1 : rows, :], stiff[0, 0:1, :]), edge.shape)
        line = lax.broadcasted_iota(jnp.int32, edge.shape, 0)
        high, low = (p.astype(jnp.float32) for p in pieces(edge))
        outs[k][2 * slots + 2] = jnp.where(line == 0, high, low).astype(jnp.bfloat16)
    for k in range(doms):
        for j in range(slots):
            outs[k][j] = tiles[send[0, 0, 0, d ^ k, j]]
    lane = lax.broadcasted_iota(jnp.int32, (rows, cells), 1)
    ends = [jnp.zeros((rows, cells), jnp.float32)] * 2
    for m in range(count + 1):
        here = stiff[0] if m == count else modes[m * rows : (m + 1) * rows, :]
        ends = [jnp.where(lane == m, end, packed) for end, packed in zip((here[:, :1], here[:, -1:]), ends)]
    if subs == 2:
        column[0] = jnp.where(lax.axis_index("sub") == 0, ends[1], ends[0])
    else:
        for side in range(2):
            column[side] = ends[side]
    for c, copy in enumerate(block_copies):
        copy.wait()
        for p in range(c * half, (c + 1) * half, 2):
            terms = pair_dot(tiles[own[0, 0, 0, p]], tiles[own[0, 0, 0, p + 1]], blocks[p : p + 2])
            for q, term in zip((p, p + 1), terms):
                sums[peer[0, 0, 0, q] * slots + slot[0, 0, 0, q]] += term
    for k in range(doms):
        for j in range(slots):
            outs[k][slots + j] = sums[(d ^ k) * slots + j].astype(jnp.bfloat16)


def turn(blocks, turned):
    for p in range(blocks.shape[0]):
        turned[p] = blocks[p].T


def stencil(subs, modes, stiff, *refs):
    columns, total = refs[:-1], refs[-1]
    rows, cells = stiff.shape[1:]
    count = modes.shape[0] // rows
    shift = helm_shift * lax.axis_index("mesh").astype(jnp.float32)
    lane = lax.broadcasted_iota(jnp.int32, (rows, cells), 1)
    line = lax.broadcasted_iota(jnp.int32, (rows, cells), 0)
    first_lane, last_lane = lane == 0, lane == cells - 1
    first_line, last_line = line == 0, line == rows - 1
    s = lax.axis_index("sub")
    if subs == 1:
        left = right = jnp.zeros(lane.shape, jnp.float32)
    elif subs == 2:
        left, right = jnp.where(s == 1, columns[0][0], 0.0), jnp.where(s == 0, columns[0][0], 0.0)
    else:
        left, right = columns[0][1], columns[1][0]

    def near_by(here, m):
        return (
            jnp.where(first_line, here, pltpu.roll(here, 1, 0)),
            jnp.where(last_line, here, pltpu.roll(here, rows - 1, 0)),
            jnp.where(first_lane, left[:, m : m + 1], pltpu.roll(here, 1, 1)),
            jnp.where(last_lane, right[:, m : m + 1], pltpu.roll(here, cells - 1, 1)),
        )

    weights = [0.5 * (stiff[0] + near) for near in near_by(stiff[0], count)]
    for m in range(count):
        here = modes[m * rows : (m + 1) * rows, :]
        result = -shift * here
        for weight, near in zip(weights, near_by(here, m)):
            result = result + weight * (here - near)
        total[pl.ds(m, rows, stride=count), :] = result


def pick(doms, slots, *refs):
    arrived, halo = dict(zip(filter(has_halo, exchange(doms)), refs)), refs[-1]
    d = lax.axis_index("dom")
    halo[...] = jnp.zeros_like(halo)
    for k, ref in arrived.items():
        for side, step in enumerate((-1, 1)):

            @pl.when(d ^ k == d + step)
            def _():
                halo[side] = ref[2 * slots : 2 * slots + PIECES]


def couple(doms, slots, own, peer, slot, send, turned, *refs):
    arrived, (_, total, out, foreign, back) = dict(zip(exchange(doms), refs)), refs[doms:]
    count = foreign.shape[1]
    rows = total.shape[0] // count
    d = lax.axis_index("dom")
    for k in range(doms):
        for j in range(slots):
            foreign[(d ^ k) * slots + j] = arrived[k][j]
            back[(d ^ k) * slots + j] = arrived[k][slots + j].astype(jnp.float32)

    def subtract(row, term):
        part = pl.ds(pl.multiple_of(row * count, count), count)
        total[part, :] -= term

    for g in range(doms):
        for j in range(slots):
            subtract(send[0, 0, 0, g, j], back[g * slots + j])
    for p in range(0, turned.shape[0], 2):
        first, second = (foreign[peer[0, 0, 0, q] * slots + slot[0, 0, 0, q]] for q in (p, p + 1))
        for q, term in zip((p, p + 1), pair_dot(first, second, turned[p : p + 2])):
            subtract(own[0, 0, 0, q], term)
    for m in range(count):
        out[m * rows : (m + 1) * rows, :] = total[pl.ds(m, rows, stride=count), :]


def finish(modes, stiff, halo, result, out, ends, sems):
    rows, cells = stiff.shape[1:]
    count = result.shape[0]
    group = ends.shape[2]
    middle = pl.ds(group, rows - 2 * group)
    copies = [pltpu.make_async_copy(result.at[:, middle], out.at[:, middle], sems.at[2])]
    copies[0].start()
    line = lax.broadcasted_iota(jnp.int32, (group, cells), 0)
    for side, (row, first) in enumerate(((0, 0), (rows - 1, rows - group))):
        near = whole(halo[side, 0], halo[side, 1])
        weight = 0.5 * (stiff[0, row : row + 1, :] + whole(halo[side, 2, 0:1], halo[side, 2, 1:2]))
        added = weight * (modes[pl.ds(row, count, stride=rows), :] - near)
        for m in range(count):
            ends[side, m] = result[m, first : first + group] + jnp.where(line == row - first, added[m : m + 1], 0.0)
        copies.append(pltpu.make_async_copy(ends.at[side], out.at[:, pl.ds(first, group)], sems.at[side]))
        copies[-1].start()
    for copy in copies:
        copy.wait()


def exchange(doms):
    if doms == 4:
        return [3, 1, 2, 0]
    return list(range(doms))


def shards(doms, subs, modes_in, stiffness, coupling, pair_own, pair_peer, pair_slot, send_rows):
    _, count, rows, cells = modes_in.shape
    slots, pairs = send_rows.shape[-1], coupling.shape[3]
    flat = modes_in.reshape(count * rows, cells)
    inputs = (pair_own, pair_peer, pair_slot, send_rows, flat, stiffness, coupling)
    *inputs, coupling = [pltpu.with_memory_space_constraint(a, pltpu.HBM) for a in inputs]
    params = pltpu.CompilerParams(vmem_limit_bytes=32 * 1024 * 1024)
    like = jax.ShapeDtypeStruct
    indices = inputs[:4]
    *outgoing, column, blocks, modes, stiff, own, peer, slot, send = pl.pallas_call(
        functools.partial(before, doms, subs, slots, rows),
        out_shape=[like((2 * slots + PIECES * has_halo(k), count, cells), jnp.bfloat16) for k in range(doms)]
        + [
            like((1 if subs == 2 else 2, rows, cells), jnp.float32),
            like((pairs, cells, cells), jnp.bfloat16),
            like(flat.shape, jnp.float32),
            like(stiffness.shape, jnp.float32),
        ]
        + [pltpu.SMEM(a.shape, a.dtype) for a in indices],
        in_specs=[HBM] * 7,
        out_specs=[VMEM] * (doms + 4) + [SMEM] * 4,
        scratch_shapes=[
            pltpu.VMEM((rows, count, cells), jnp.bfloat16),
            pltpu.VMEM((doms * slots, count, cells), jnp.float32),
            pltpu.SemaphoreType.DMA((len(inputs),)),
            pltpu.SemaphoreType.DMA((2,)),
        ],
        compiler_params=params,
        name="before",
    )(*inputs, coupling)
    indices = [pltpu.with_memory_space_constraint(a, pltpu.SMEM) for a in (own, peer, slot, send)]
    arrived = {}
    for k in exchange(doms):
        route = [(2 * d + h, 2 * (d ^ k) + 1 - h) for d in range(doms) for h in range(2)]
        arrived[k] = lax.ppermute(outgoing[k], ("dom", "mesh"), route)
    if subs == 1:
        columns = []
    elif subs == 2:
        columns = [lax.ppermute(column, "sub", [(0, 1), (1, 0)])]
    else:
        columns = [
            lax.ppermute(column, "sub", [(i, i + 1) for i in range(subs - 1)]),
            lax.ppermute(column, "sub", [(i + 1, i) for i in range(subs - 1)]),
        ]
    cost = pl.CostEstimate(flops=0, bytes_accessed=8 << 20, transcendentals=0)
    turned = pl.pallas_call(
        turn,
        out_shape=like(blocks.shape, blocks.dtype),
        in_specs=[VMEM],
        out_specs=VMEM,
        compiler_params=params,
        cost_estimate=cost,
        name="turn",
    )(blocks)
    partial = pl.pallas_call(
        functools.partial(stencil, subs),
        out_shape=like(flat.shape, jnp.float32),
        in_specs=[VMEM] * (2 + len(columns)),
        out_specs=VMEM,
        compiler_params=params,
        name="stencil",
    )(modes, stiff, *columns)
    halo = pl.pallas_call(
        functools.partial(pick, doms, slots),
        out_shape=like((2, PIECES, count, cells), jnp.bfloat16),
        in_specs=[VMEM] * sum(map(has_halo, range(doms))) + [ANY] * 2,
        out_specs=VMEM,
        compiler_params=params,
        name="pick",
    )(*(arrived[k] for k in exchange(doms) if has_halo(k)), turned, partial)
    halo = lax.ppermute(halo, "mesh", [(0, 1), (1, 0)])
    _, result = pl.pallas_call(
        functools.partial(couple, doms, slots),
        out_shape=[like(partial.shape, partial.dtype)] * 2,
        in_specs=[SMEM] * 4 + [VMEM] * (2 + doms),
        out_specs=[VMEM] * 2,
        scratch_shapes=[
            pltpu.VMEM((doms * slots, count, cells), jnp.bfloat16),
            pltpu.VMEM((doms * slots, count, cells), jnp.float32),
        ],
        input_output_aliases={5 + doms: 0},
        compiler_params=params,
        cost_estimate=cost,
        name="couple",
    )(*indices, turned, *(arrived[k] for k in exchange(doms)), partial)
    out = pl.pallas_call(
        finish,
        out_shape=like((count, rows, cells), jnp.float32),
        in_specs=[VMEM] * 4,
        out_specs=HBM,
        scratch_shapes=[pltpu.VMEM((2, count, 8, cells), jnp.float32), pltpu.SemaphoreType.DMA((3,))],
        compiler_params=params,
        name="finish",
    )(modes, stiff, halo, result.reshape(count, rows, cells))
    return out.reshape(modes_in.shape)


def solution(mesh):
    return jax.shard_map(
        functools.partial(shards, mesh.shape["dom"], mesh.shape["sub"]),
        mesh=mesh,
        in_specs=(
            P("mesh", "copies", "dom", "sub"),
            P(("copies", "mesh"), "dom", "sub"),
            P("mesh", "dom", "sub", None, None, None),
            P("mesh", "dom", "sub", None),
            P("mesh", "dom", "sub", None),
            P("mesh", "dom", "sub", None),
            P("mesh", "dom", "sub", None, None),
        ),
        out_specs=P("mesh", "copies", "dom", "sub"),
        check_vma=False,
    )
```

```python
import functools

import jax
import jax.numpy as jnp
from jax import lax
from jax.experimental import pallas as pl
from jax.experimental.pallas import tpu as pltpu
from jax.sharding import PartitionSpec as P

helm_shift = 1.0
PIECES = 3
SMEM = pl.BlockSpec(memory_space=pltpu.SMEM)
VMEM = pl.BlockSpec(memory_space=pltpu.VMEM)
ANY = pl.BlockSpec(memory_space=pl.ANY)
HBM = pl.BlockSpec(memory_space=pltpu.HBM)


def has_halo(k):
    return k > 0 and k & (k + 1) == 0


def pieces(x):
    high = x.astype(jnp.bfloat16)
    return high, (x - high.astype(jnp.float32)).astype(jnp.bfloat16)


def whole(high, low):
    return high.astype(jnp.float32) + low.astype(jnp.float32)


def pair_dot(a, b, blocks):
    none = jnp.zeros_like(a)
    rows = jnp.concatenate([jnp.concatenate([a, none], 1), jnp.concatenate([none, b], 1)], 0)
    both = jnp.dot(rows, blocks.reshape(2 * blocks.shape[1], -1), preferred_element_type=jnp.float32)
    return both[: a.shape[0]], both[a.shape[0] :]


def load(sources, targets, sems, priority=0):
    copies = [pltpu.make_async_copy(a, b, sems.at[i]) for i, (a, b) in enumerate(zip(sources, targets))]
    for copy in copies:
        copy.start(priority=priority)
    return copies


def before(doms, subs, slots, rows, own_in, peer_in, slot_in, send_in, modes_in, stiff_in, coupling, *refs):
    outs, (column, blocks, modes, stiff) = refs[:doms], refs[doms : doms + 4]
    own, peer, slot, send, tiles, sums, sems, block_sems = refs[doms + 4 :]
    sources = (own_in, peer_in, slot_in, send_in, modes_in, stiff_in)
    copies = load(sources, (own, peer, slot, send, modes, stiff), sems)
    half = blocks.shape[0] // 2
    parts = [pl.ds(0, half), pl.ds(half, half)]
    block_copies = load([coupling.at[0, 0, 0, part] for part in parts], [blocks.at[part] for part in parts], block_sems, 1)
    d = lax.axis_index("dom")
    count, cells = tiles.shape[1:]
    sums[...] = jnp.zeros_like(sums)
    for copy in copies:
        copy.wait()
    for r in range(rows):
        tiles[r] = modes[pl.ds(r, count, stride=rows), :].astype(jnp.bfloat16)

    for k in filter(has_halo, range(doms)):
        last = d ^ k > d
        edge = jnp.where(last, modes[pl.ds(rows - 1, count, stride=rows), :], modes[pl.ds(0, count, stride=rows), :])
        for i, piece in enumerate(pieces(edge)):
            outs[k][2 * slots + i] = piece
        edge = jnp.broadcast_to(jnp.where(last, stiff[0, rows - 1 : rows, :], stiff[0, 0:1, :]), edge.shape)
        line = lax.broadcasted_iota(jnp.int32, edge.shape, 0)
        high, low = (p.astype(jnp.float32) for p in pieces(edge))
        outs[k][2 * slots + 2] = jnp.where(line == 0, high, low).astype(jnp.bfloat16)
    for k in range(doms):
        for j in range(slots):
            outs[k][j] = tiles[send[0, 0, 0, d ^ k, j]]
    lane = lax.broadcasted_iota(jnp.int32, (rows, cells), 1)
    ends = [jnp.zeros((rows, cells), jnp.float32)] * 2
    for m in range(count + 1):
        here = stiff[0] if m == count else modes[m * rows : (m + 1) * rows, :]
        ends = [jnp.where(lane == m, end, packed) for end, packed in zip((here[:, :1], here[:, -1:]), ends)]
    if subs == 2:
        column[0] = jnp.zeros_like(column[0])
        column[0, :rows] = jnp.where(lax.axis_index("sub") == 0, ends[1], ends[0])
    else:
        for side in range(2):
            column[side] = ends[side]
    for c, copy in enumerate(block_copies):
        copy.wait()
        for p in range(c * half, (c + 1) * half, 2):
            terms = pair_dot(tiles[own[0, 0, 0, p]], tiles[own[0, 0, 0, p + 1]], blocks[p : p + 2])
            for q, term in zip((p, p + 1), terms):
                sums[peer[0, 0, 0, q] * slots + slot[0, 0, 0, q]] += term
    for k in range(doms):
        for j in range(slots):
            outs[k][slots + j] = sums[(d ^ k) * slots + j].astype(jnp.bfloat16)


def turn(blocks, turned):
    for p in range(blocks.shape[0]):
        turned[p] = blocks[p].T


def stencil(subs, modes, stiff, _, *refs):
    columns, total = refs[:-1], refs[-1]
    rows, cells = stiff.shape[1:]
    count = modes.shape[0] // rows
    shift = helm_shift * lax.axis_index("mesh").astype(jnp.float32)
    lane = lax.broadcasted_iota(jnp.int32, (rows, cells), 1)
    line = lax.broadcasted_iota(jnp.int32, (rows, cells), 0)
    first_lane, last_lane = lane == 0, lane == cells - 1
    first_line, last_line = line == 0, line == rows - 1
    s = lax.axis_index("sub")
    if subs == 1:
        left = right = jnp.zeros(lane.shape, jnp.float32)
    elif subs == 2:
        left, right = jnp.where(s == 1, columns[0][0, :rows], 0.0), jnp.where(s == 0, columns[0][0, :rows], 0.0)
    else:
        left, right = columns[0][1], columns[1][0]

    def near_by(here, m):
        return (
            jnp.where(first_line, here, pltpu.roll(here, 1, 0)),
            jnp.where(last_line, here, pltpu.roll(here, rows - 1, 0)),
            jnp.where(first_lane, left[:, m : m + 1], pltpu.roll(here, 1, 1)),
            jnp.where(last_lane, right[:, m : m + 1], pltpu.roll(here, cells - 1, 1)),
        )

    weights = [0.5 * (stiff[0] + near) for near in near_by(stiff[0], count)]
    for m in range(count):
        here = modes[m * rows : (m + 1) * rows, :]
        result = -shift * here
        for weight, near in zip(weights, near_by(here, m)):
            result = result + weight * (here - near)
        total[pl.ds(m, rows, stride=count), :] = result


def pick(doms, slots, *refs):
    arrived, halo = dict(zip(filter(has_halo, exchange(doms)), refs)), refs[-1]
    d = lax.axis_index("dom")
    halo[...] = jnp.zeros_like(halo)
    for k, ref in arrived.items():
        for side, step in enumerate((-1, 1)):

            @pl.when(d ^ k == d + step)
            def _():
                halo[side] = ref[2 * slots : 2 * slots + PIECES]


def couple(doms, slots, own, peer, slot, send, turned, modes, stiff, halo, *refs):
    arrived, (_, total, out, foreign, back, held, sems) = dict(zip(exchange(doms), refs)), refs[doms:]
    count = foreign.shape[1]
    rows = total.shape[0] // count
    d = lax.axis_index("dom")
    for k in range(doms):
        for j in range(slots):
            foreign[(d ^ k) * slots + j] = arrived[k][j]
            back[(d ^ k) * slots + j] = arrived[k][slots + j].astype(jnp.float32)
    for side, row in enumerate((0, rows - 1)):
        near = whole(halo[side, 0], halo[side, 1])
        weight = 0.5 * (stiff[0, row : row + 1, :] + whole(halo[side, 2, 0:1], halo[side, 2, 1:2]))
        total[row * count : (row + 1) * count, :] += weight * (modes[pl.ds(row, count, stride=rows), :] - near)

    def subtract(row, term):
        part = pl.ds(pl.multiple_of(row * count, count), count)
        total[part, :] -= term

    for g in range(doms):
        for j in range(slots):
            subtract(send[0, 0, 0, g, j], back[g * slots + j])
    for p in range(0, turned.shape[0], 2):
        first, second = (foreign[peer[0, 0, 0, q] * slots + slot[0, 0, 0, q]] for q in (p, p + 1))
        for q, term in zip((p, p + 1), pair_dot(first, second, turned[p : p + 2])):
            subtract(own[0, 0, 0, q], term)
    copies = []
    for i in range(2):
        some = range(i * count // 2, (i + 1) * count // 2)
        for m in some:
            held[m * rows : (m + 1) * rows, :] = total[pl.ds(m, rows, stride=count), :]
        part = pl.ds(some[0] * rows, len(some) * rows)
        copies.append(pltpu.make_async_copy(held.at[part], out.at[part], sems.at[i]))
        copies[-1].start()
    for copy in copies:
        copy.wait()


def exchange(doms):
    if doms == 4:
        return [3, 1, 2, 0]
    return list(range(doms))


def shards(doms, subs, modes_in, stiffness, coupling, pair_own, pair_peer, pair_slot, send_rows):
    _, count, rows, cells = modes_in.shape
    slots, pairs = send_rows.shape[-1], coupling.shape[3]
    flat = modes_in.reshape(count * rows, cells)
    inputs = (pair_own, pair_peer, pair_slot, send_rows, flat, stiffness, coupling)
    *inputs, coupling = [pltpu.with_memory_space_constraint(a, pltpu.HBM) for a in inputs]
    params = pltpu.CompilerParams(vmem_limit_bytes=32 * 1024 * 1024)
    like = jax.ShapeDtypeStruct
    indices = inputs[:4]
    *outgoing, column, blocks, modes, stiff, own, peer, slot, send = pl.pallas_call(
        functools.partial(before, doms, subs, slots, rows),
        out_shape=[like((2 * slots + PIECES * has_halo(k), count, cells), jnp.bfloat16) for k in range(doms)]
        + [
            like((1, (slots + 1) * count, cells) if subs == 2 else (2, rows, cells), jnp.float32),
            like((pairs, cells, cells), jnp.bfloat16),
            like(flat.shape, jnp.float32),
            like(stiffness.shape, jnp.float32),
        ]
        + [pltpu.SMEM(a.shape, a.dtype) for a in indices],
        in_specs=[HBM] * 7,
        out_specs=[VMEM] * (doms + 4) + [SMEM] * 4,
        scratch_shapes=[
            pltpu.VMEM((rows, count, cells), jnp.bfloat16),
            pltpu.VMEM((doms * slots, count, cells), jnp.float32),
            pltpu.SemaphoreType.DMA((len(inputs),)),
            pltpu.SemaphoreType.DMA((2,)),
        ],
        compiler_params=params,
        name="before",
    )(*inputs, coupling)
    indices = [pltpu.with_memory_space_constraint(a, pltpu.SMEM) for a in (own, peer, slot, send)]
    arrived = {}
    for k in exchange(doms):
        route = [(2 * d + h, 2 * (d ^ k) + 1 - h) for d in range(doms) for h in range(2)]
        arrived[k] = lax.ppermute(outgoing[k], ("dom", "mesh"), route)
    if subs == 1:
        columns = []
    elif subs == 2:
        columns = [lax.ppermute(column, "sub", [(0, 1), (1, 0)])]
    else:
        columns = [
            lax.ppermute(column, "sub", [(i, i + 1) for i in range(subs - 1)]),
            lax.ppermute(column, "sub", [(i + 1, i) for i in range(subs - 1)]),
        ]
    cost = pl.CostEstimate(flops=0, bytes_accessed=8 << 20, transcendentals=0)
    turned = pl.pallas_call(
        turn,
        out_shape=like(blocks.shape, blocks.dtype),
        in_specs=[VMEM],
        out_specs=VMEM,
        compiler_params=params,
        cost_estimate=cost,
        name="turn",
    )(blocks)
    picked = pl.pallas_call(
        functools.partial(pick, doms, slots),
        out_shape=like((2, PIECES, count, cells), jnp.bfloat16),
        in_specs=[VMEM] * sum(map(has_halo, range(doms))) + [ANY],
        out_specs=VMEM,
        compiler_params=params,
        name="pick",
    )(*(arrived[k] for k in exchange(doms) if has_halo(k)), turned)
    partial = pl.pallas_call(
        functools.partial(stencil, subs),
        out_shape=like(flat.shape, jnp.float32),
        in_specs=[VMEM, VMEM, ANY] + [VMEM] * len(columns),
        out_specs=VMEM,
        compiler_params=params,
        name="stencil",
    )(modes, stiff, picked, *columns)
    halo = lax.ppermute(picked, "mesh", [(0, 1), (1, 0)])
    _, out = pl.pallas_call(
        functools.partial(couple, doms, slots),
        out_shape=[like(partial.shape, partial.dtype)] * 2,
        in_specs=[SMEM] * 4 + [VMEM] * (5 + doms),
        out_specs=[VMEM, HBM],
        scratch_shapes=[
            pltpu.VMEM((doms * slots, count, cells), jnp.bfloat16),
            pltpu.VMEM((doms * slots, count, cells), jnp.float32),
            pltpu.VMEM(flat.shape, jnp.float32),
            pltpu.SemaphoreType.DMA((2,)),
        ],
        input_output_aliases={8 + doms: 0},
        compiler_params=params,
        cost_estimate=cost,
        name="couple",
    )(*indices, turned, modes, stiff, halo, *(arrived[k] for k in exchange(doms)), partial)
    return out.reshape(modes_in.shape)


def solution(mesh):
    return jax.shard_map(
        functools.partial(shards, mesh.shape["dom"], mesh.shape["sub"]),
        mesh=mesh,
        in_specs=(
            P("mesh", "copies", "dom", "sub"),
            P(("copies", "mesh"), "dom", "sub"),
            P("mesh", "dom", "sub", None, None, None),
            P("mesh", "dom", "sub", None),
            P("mesh", "dom", "sub", None),
            P("mesh", "dom", "sub", None),
            P("mesh", "dom", "sub", None, None),
        ),
        out_specs=P("mesh", "copies", "dom", "sub"),
        check_vma=False,
    )
```

```python
import functools

import jax
import jax.numpy as jnp
from jax import lax
from jax.experimental import pallas as pl
from jax.experimental.pallas import tpu as pltpu
from jax.sharding import PartitionSpec as P

helm_shift = 1.0
PIECES = 3
SMEM = pl.BlockSpec(memory_space=pltpu.SMEM)
VMEM = pl.BlockSpec(memory_space=pltpu.VMEM)
ANY = pl.BlockSpec(memory_space=pl.ANY)
HBM = pl.BlockSpec(memory_space=pltpu.HBM)


def has_halo(k):
    return k > 0 and k & (k + 1) == 0


def pieces(x):
    high = x.astype(jnp.bfloat16)
    return high, (x - high.astype(jnp.float32)).astype(jnp.bfloat16)


def whole(high, low):
    return high.astype(jnp.float32) + low.astype(jnp.float32)


def pair_dot(a, b, blocks):
    none = jnp.zeros_like(a)
    rows = jnp.concatenate([jnp.concatenate([a, none], 1), jnp.concatenate([none, b], 1)], 0)
    both = jnp.dot(rows, blocks.reshape(2 * blocks.shape[1], -1), preferred_element_type=jnp.float32)
    return both[: a.shape[0]], both[a.shape[0] :]


def load(sources, targets, sems, priority=0):
    copies = [pltpu.make_async_copy(a, b, sems.at[i]) for i, (a, b) in enumerate(zip(sources, targets))]
    for copy in copies:
        copy.start(priority=priority)
    return copies


def before(doms, subs, slots, rows, own_in, peer_in, slot_in, send_in, modes_in, stiff_in, coupling, *refs):
    outs, (column, blocks, modes, stiff) = refs[:doms], refs[doms : doms + 4]
    own, peer, slot, send, tiles, sums, sems, block_sems = refs[doms + 4 :]
    sources = (own_in, peer_in, slot_in, send_in, modes_in, stiff_in)
    copies = load(sources, (own, peer, slot, send, modes, stiff), sems)
    half = blocks.shape[0] // 2
    parts = [pl.ds(0, half), pl.ds(half, half)]
    block_copies = load([coupling.at[0, 0, 0, part] for part in parts], [blocks.at[part] for part in parts], block_sems, 1)
    d = lax.axis_index("dom")
    count, cells = tiles.shape[1:]
    sums[...] = jnp.zeros_like(sums)
    for copy in copies:
        copy.wait()
    for r in range(rows):
        tiles[r] = modes[pl.ds(r, count, stride=rows), :].astype(jnp.bfloat16)

    for k in filter(has_halo, range(doms)):
        last = d ^ k > d
        edge = jnp.where(last, modes[pl.ds(rows - 1, count, stride=rows), :], modes[pl.ds(0, count, stride=rows), :])
        for i, piece in enumerate(pieces(edge)):
            outs[k][2 * slots + i] = piece
        edge = jnp.broadcast_to(jnp.where(last, stiff[0, rows - 1 : rows, :], stiff[0, 0:1, :]), edge.shape)
        line = lax.broadcasted_iota(jnp.int32, edge.shape, 0)
        high, low = (p.astype(jnp.float32) for p in pieces(edge))
        outs[k][2 * slots + 2] = jnp.where(line == 0, high, low).astype(jnp.bfloat16)
    for k in range(doms):
        for j in range(slots):
            outs[k][j] = tiles[send[0, 0, 0, d ^ k, j]]
    lane = lax.broadcasted_iota(jnp.int32, (rows, cells), 1)
    ends = [jnp.zeros((rows, cells), jnp.float32)] * 2
    for m in range(count + 1):
        here = stiff[0] if m == count else modes[m * rows : (m + 1) * rows, :]
        ends = [jnp.where(lane == m, end, packed) for end, packed in zip((here[:, :1], here[:, -1:]), ends)]
    if subs == 2:
        column[0] = jnp.zeros_like(column[0])
        column[0, :rows] = jnp.where(lax.axis_index("sub") == 0, ends[1], ends[0])
    else:
        for side in range(2):
            column[side] = ends[side]
    for c, copy in enumerate(block_copies):
        copy.wait()
        for p in range(c * half, (c + 1) * half, 2):
            terms = pair_dot(tiles[own[0, 0, 0, p]], tiles[own[0, 0, 0, p + 1]], blocks[p : p + 2])
            for q, term in zip((p, p + 1), terms):
                sums[peer[0, 0, 0, q] * slots + slot[0, 0, 0, q]] += term
    for k in range(doms):
        for j in range(slots):
            outs[k][slots + j] = sums[(d ^ k) * slots + j].astype(jnp.bfloat16)


def turn(blocks, turned):
    for p in range(blocks.shape[0]):
        turned[p] = blocks[p].T


def stencil(doms, subs, slots, send, modes, stiff, _, *refs):
    early = [k for k in exchange(doms) if has_halo(k)]
    arrived, columns, total = refs[: len(early)], refs[len(early) : -1], refs[-1]
    rows, cells = stiff.shape[1:]
    count = modes.shape[0] // rows
    shift = helm_shift * lax.axis_index("mesh").astype(jnp.float32)
    lane = lax.broadcasted_iota(jnp.int32, (rows, cells), 1)
    line = lax.broadcasted_iota(jnp.int32, (rows, cells), 0)
    first_lane, last_lane = lane == 0, lane == cells - 1
    first_line, last_line = line == 0, line == rows - 1
    s = lax.axis_index("sub")
    if subs == 1:
        left = right = jnp.zeros(lane.shape, jnp.float32)
    elif subs == 2:
        left, right = jnp.where(s == 1, columns[0][0, :rows], 0.0), jnp.where(s == 0, columns[0][0, :rows], 0.0)
    else:
        left, right = columns[0][1], columns[1][0]

    def near_by(here, m):
        return (
            jnp.where(first_line, here, pltpu.roll(here, 1, 0)),
            jnp.where(last_line, here, pltpu.roll(here, rows - 1, 0)),
            jnp.where(first_lane, left[:, m : m + 1], pltpu.roll(here, 1, 1)),
            jnp.where(last_lane, right[:, m : m + 1], pltpu.roll(here, cells - 1, 1)),
        )

    weights = [0.5 * (stiff[0] + near) for near in near_by(stiff[0], count)]
    for m in range(count):
        here = modes[m * rows : (m + 1) * rows, :]
        result = -shift * here
        for weight, near in zip(weights, near_by(here, m)):
            result = result + weight * (here - near)
        total[pl.ds(m, rows, stride=count), :] = result
    take_back(lax.axis_index("dom"), count, slots, send, total, zip(early, arrived))


def take_back(d, count, slots, send, total, arrived):
    for k, ref in arrived:
        for j in range(slots):
            part = pl.ds(pl.multiple_of(send[0, 0, 0, d ^ k, j] * count, count), count)
            total[part, :] -= ref[slots + j].astype(jnp.float32)


def pick(doms, slots, *refs):
    arrived, halo = dict(zip(filter(has_halo, exchange(doms)), refs)), refs[-1]
    d = lax.axis_index("dom")
    halo[...] = jnp.zeros_like(halo)
    for k, ref in arrived.items():
        for side, step in enumerate((-1, 1)):

            @pl.when(d ^ k == d + step)
            def _():
                halo[side] = ref[2 * slots : 2 * slots + PIECES]


def couple(doms, slots, own, peer, slot, send, turned, modes, stiff, halo, *refs):
    arrived, (_, total, out, foreign, held, sems) = dict(zip(exchange(doms), refs)), refs[doms:]
    count = foreign.shape[1]
    rows = total.shape[0] // count
    d = lax.axis_index("dom")
    for k in range(doms):
        for j in range(slots):
            foreign[(d ^ k) * slots + j] = arrived[k][j]
    for side, row in enumerate((0, rows - 1)):
        near = whole(halo[side, 0], halo[side, 1])
        weight = 0.5 * (stiff[0, row : row + 1, :] + whole(halo[side, 2, 0:1], halo[side, 2, 1:2]))
        total[row * count : (row + 1) * count, :] += weight * (modes[pl.ds(row, count, stride=rows), :] - near)

    def subtract(row, term):
        part = pl.ds(pl.multiple_of(row * count, count), count)
        total[part, :] -= term

    take_back(d, count, slots, send, total, ((k, arrived[k]) for k in range(doms) if not has_halo(k)))
    for p in range(0, turned.shape[0], 2):
        first, second = (foreign[peer[0, 0, 0, q] * slots + slot[0, 0, 0, q]] for q in (p, p + 1))
        for q, term in zip((p, p + 1), pair_dot(first, second, turned[p : p + 2])):
            subtract(own[0, 0, 0, q], term)
    copies = []
    for i in range(2):
        some = range(i * count // 2, (i + 1) * count // 2)
        for m in some:
            held[m * rows : (m + 1) * rows, :] = total[pl.ds(m, rows, stride=count), :]
        part = pl.ds(some[0] * rows, len(some) * rows)
        copies.append(pltpu.make_async_copy(held.at[part], out.at[part], sems.at[i]))
        copies[-1].start()
    for copy in copies:
        copy.wait()


def exchange(doms):
    if doms == 4:
        return [3, 1, 2, 0]
    return list(range(doms))


def shards(doms, subs, modes_in, stiffness, coupling, pair_own, pair_peer, pair_slot, send_rows):
    _, count, rows, cells = modes_in.shape
    slots, pairs = send_rows.shape[-1], coupling.shape[3]
    flat = modes_in.reshape(count * rows, cells)
    inputs = (pair_own, pair_peer, pair_slot, send_rows, flat, stiffness, coupling)
    *inputs, coupling = [pltpu.with_memory_space_constraint(a, pltpu.HBM) for a in inputs]
    params = pltpu.CompilerParams(vmem_limit_bytes=32 * 1024 * 1024)
    like = jax.ShapeDtypeStruct
    indices = inputs[:4]
    *outgoing, column, blocks, modes, stiff, own, peer, slot, send = pl.pallas_call(
        functools.partial(before, doms, subs, slots, rows),
        out_shape=[like((2 * slots + PIECES * has_halo(k), count, cells), jnp.bfloat16) for k in range(doms)]
        + [
            like((1, (slots + 1) * count, cells) if subs == 2 else (2, rows, cells), jnp.float32),
            like((pairs, cells, cells), jnp.bfloat16),
            like(flat.shape, jnp.float32),
            like(stiffness.shape, jnp.float32),
        ]
        + [pltpu.SMEM(a.shape, a.dtype) for a in indices],
        in_specs=[HBM] * 7,
        out_specs=[VMEM] * (doms + 4) + [SMEM] * 4,
        scratch_shapes=[
            pltpu.VMEM((rows, count, cells), jnp.bfloat16),
            pltpu.VMEM((doms * slots, count, cells), jnp.float32),
            pltpu.SemaphoreType.DMA((len(inputs),)),
            pltpu.SemaphoreType.DMA((2,)),
        ],
        compiler_params=params,
        name="before",
    )(*inputs, coupling)
    indices = [pltpu.with_memory_space_constraint(a, pltpu.SMEM) for a in (own, peer, slot, send)]
    arrived = {}
    for k in exchange(doms):
        route = [(2 * d + h, 2 * (d ^ k) + 1 - h) for d in range(doms) for h in range(2)]
        arrived[k] = lax.ppermute(outgoing[k], ("dom", "mesh"), route)
    if subs == 1:
        columns = []
    elif subs == 2:
        columns = [lax.ppermute(column, "sub", [(0, 1), (1, 0)])]
    else:
        columns = [
            lax.ppermute(column, "sub", [(i, i + 1) for i in range(subs - 1)]),
            lax.ppermute(column, "sub", [(i + 1, i) for i in range(subs - 1)]),
        ]
    cost = pl.CostEstimate(flops=0, bytes_accessed=8 << 20, transcendentals=0)
    turned = pl.pallas_call(
        turn,
        out_shape=like(blocks.shape, blocks.dtype),
        in_specs=[VMEM],
        out_specs=VMEM,
        compiler_params=params,
        cost_estimate=cost,
        name="turn",
    )(blocks)
    picked = pl.pallas_call(
        functools.partial(pick, doms, slots),
        out_shape=like((2, PIECES, count, cells), jnp.bfloat16),
        in_specs=[VMEM] * sum(map(has_halo, range(doms))) + [ANY],
        out_specs=VMEM,
        compiler_params=params,
        name="pick",
    )(*(arrived[k] for k in exchange(doms) if has_halo(k)), turned)
    partial = pl.pallas_call(
        functools.partial(stencil, doms, subs, slots),
        out_shape=like(flat.shape, jnp.float32),
        in_specs=[SMEM, VMEM, VMEM, ANY] + [VMEM] * (sum(map(has_halo, range(doms))) + len(columns)),
        out_specs=VMEM,
        compiler_params=params,
        name="stencil",
    )(indices[3], modes, stiff, picked, *(arrived[k] for k in exchange(doms) if has_halo(k)), *columns)
    halo = lax.ppermute(picked, "mesh", [(0, 1), (1, 0)])
    _, out = pl.pallas_call(
        functools.partial(couple, doms, slots),
        out_shape=[like(partial.shape, partial.dtype)] * 2,
        in_specs=[SMEM] * 4 + [VMEM] * (5 + doms),
        out_specs=[VMEM, HBM],
        scratch_shapes=[
            pltpu.VMEM((doms * slots, count, cells), jnp.bfloat16),
            pltpu.VMEM(flat.shape, jnp.float32),
            pltpu.SemaphoreType.DMA((2,)),
        ],
        input_output_aliases={8 + doms: 0},
        compiler_params=params,
        cost_estimate=cost,
        name="couple",
    )(*indices, turned, modes, stiff, halo, *(arrived[k] for k in exchange(doms)), partial)
    return out.reshape(modes_in.shape)


def solution(mesh):
    return jax.shard_map(
        functools.partial(shards, mesh.shape["dom"], mesh.shape["sub"]),
        mesh=mesh,
        in_specs=(
            P("mesh", "copies", "dom", "sub"),
            P(("copies", "mesh"), "dom", "sub"),
            P("mesh", "dom", "sub", None, None, None),
            P("mesh", "dom", "sub", None),
            P("mesh", "dom", "sub", None),
            P("mesh", "dom", "sub", None),
            P("mesh", "dom", "sub", None, None),
        ),
        out_specs=P("mesh", "copies", "dom", "sub"),
        check_vma=False,
    )
```

```python
import functools

import jax
import jax.numpy as jnp
from jax import lax
from jax.experimental import pallas as pl
from jax.experimental.pallas import tpu as pltpu
from jax.sharding import PartitionSpec as P

helm_shift = 1.0
PIECES = 3
SMEM = pl.BlockSpec(memory_space=pltpu.SMEM)
VMEM = pl.BlockSpec(memory_space=pltpu.VMEM)
ANY = pl.BlockSpec(memory_space=pl.ANY)
HBM = pl.BlockSpec(memory_space=pltpu.HBM)


def has_halo(k):
    return k > 0 and k & (k + 1) == 0


def pieces(x):
    high = x.astype(jnp.bfloat16)
    return high, (x - high.astype(jnp.float32)).astype(jnp.bfloat16)


def whole(high, low):
    return high.astype(jnp.float32) + low.astype(jnp.float32)


def pair_dot(a, b, blocks):
    none = jnp.zeros_like(a)
    rows = jnp.concatenate([jnp.concatenate([a, none], 1), jnp.concatenate([none, b], 1)], 0)
    both = jnp.dot(rows, blocks.reshape(2 * blocks.shape[1], -1), preferred_element_type=jnp.float32)
    return both[: a.shape[0]], both[a.shape[0] :]


def load(sources, targets, sems, priority=0):
    copies = [pltpu.make_async_copy(a, b, sems.at[i]) for i, (a, b) in enumerate(zip(sources, targets))]
    for copy in copies:
        copy.start(priority=priority)
    return copies


def before(doms, subs, slots, rows, own_in, peer_in, slot_in, send_in, modes_in, stiff_in, coupling, *refs):
    outs, (column, blocks, modes, stiff) = refs[:doms], refs[doms : doms + 4]
    own, peer, slot, send, tiles, sums, sems, block_sems = refs[doms + 4 :]
    sources = (own_in, peer_in, slot_in, send_in, modes_in, stiff_in)
    copies = load(sources, (own, peer, slot, send, modes, stiff), sems)
    pairs = blocks.shape[0]
    cuts = (0, pairs // 2 + 4, pairs)
    parts = [pl.ds(a, b - a) for a, b in zip(cuts, cuts[1:])]
    block_copies = load([coupling.at[0, 0, 0, part] for part in parts], [blocks.at[part] for part in parts], block_sems, 1)
    d = lax.axis_index("dom")
    count, cells = tiles.shape[1:]
    sums[...] = jnp.zeros_like(sums)
    for copy in copies:
        copy.wait()
    for r in range(rows):
        tiles[r] = modes[pl.ds(r, count, stride=rows), :].astype(jnp.bfloat16)

    for k in filter(has_halo, range(doms)):
        last = d ^ k > d
        edge = jnp.where(last, modes[pl.ds(rows - 1, count, stride=rows), :], modes[pl.ds(0, count, stride=rows), :])
        for i, piece in enumerate(pieces(edge)):
            outs[k][2 * slots + i] = piece
        edge = jnp.broadcast_to(jnp.where(last, stiff[0, rows - 1 : rows, :], stiff[0, 0:1, :]), edge.shape)
        line = lax.broadcasted_iota(jnp.int32, edge.shape, 0)
        high, low = (p.astype(jnp.float32) for p in pieces(edge))
        outs[k][2 * slots + 2] = jnp.where(line == 0, high, low).astype(jnp.bfloat16)
    for k in range(doms):
        for j in range(slots):
            outs[k][j] = tiles[send[0, 0, 0, d ^ k, j]]
    lane = lax.broadcasted_iota(jnp.int32, (rows, cells), 1)
    ends = [jnp.zeros((rows, cells), jnp.float32)] * 2
    for m in range(count + 1):
        here = stiff[0] if m == count else modes[m * rows : (m + 1) * rows, :]
        ends = [jnp.where(lane == m, end, packed) for end, packed in zip((here[:, :1], here[:, -1:]), ends)]
    if subs == 2:
        column[0] = jnp.zeros_like(column[0])
        column[0, :rows] = jnp.where(lax.axis_index("sub") == 0, ends[1], ends[0])
    else:
        for side in range(2):
            column[side] = ends[side]
    for c, copy in enumerate(block_copies):
        copy.wait()
        for p in range(cuts[c], cuts[c + 1], 2):
            terms = pair_dot(tiles[own[0, 0, 0, p]], tiles[own[0, 0, 0, p + 1]], blocks[p : p + 2])
            for q, term in zip((p, p + 1), terms):
                sums[peer[0, 0, 0, q] * slots + slot[0, 0, 0, q]] += term
    for k in range(doms):
        for j in range(slots):
            outs[k][slots + j] = sums[(d ^ k) * slots + j].astype(jnp.bfloat16)


def turn(blocks, turned):
    for p in range(blocks.shape[0]):
        turned[p] = blocks[p].T


def stencil(doms, subs, slots, send, modes, stiff, _, *refs):
    early = [k for k in exchange(doms) if has_halo(k)]
    arrived, columns, total = refs[: len(early)], refs[len(early) : -1], refs[-1]
    rows, cells = stiff.shape[1:]
    count = modes.shape[0] // rows
    shift = helm_shift * lax.axis_index("mesh").astype(jnp.float32)
    lane = lax.broadcasted_iota(jnp.int32, (rows, cells), 1)
    line = lax.broadcasted_iota(jnp.int32, (rows, cells), 0)
    first_lane, last_lane = lane == 0, lane == cells - 1
    first_line, last_line = line == 0, line == rows - 1
    s = lax.axis_index("sub")
    if subs == 1:
        left = right = jnp.zeros(lane.shape, jnp.float32)
    elif subs == 2:
        left, right = jnp.where(s == 1, columns[0][0, :rows], 0.0), jnp.where(s == 0, columns[0][0, :rows], 0.0)
    else:
        left, right = columns[0][1], columns[1][0]

    def near_by(here, m):
        return (
            jnp.where(first_line, here, pltpu.roll(here, 1, 0)),
            jnp.where(last_line, here, pltpu.roll(here, rows - 1, 0)),
            jnp.where(first_lane, left[:, m : m + 1], pltpu.roll(here, 1, 1)),
            jnp.where(last_lane, right[:, m : m + 1], pltpu.roll(here, cells - 1, 1)),
        )

    weights = [0.5 * (stiff[0] + near) for near in near_by(stiff[0], count)]
    for m in range(count):
        here = modes[m * rows : (m + 1) * rows, :]
        result = -shift * here
        for weight, near in zip(weights, near_by(here, m)):
            result = result + weight * (here - near)
        total[pl.ds(m, rows, stride=count), :] = result
    take_back(lax.axis_index("dom"), count, slots, send, total, zip(early, arrived))


def take_back(d, count, slots, send, total, arrived):
    for k, ref in arrived:
        for j in range(slots):
            part = pl.ds(pl.multiple_of(send[0, 0, 0, d ^ k, j] * count, count), count)
            total[part, :] -= ref[slots + j].astype(jnp.float32)


def pick(doms, slots, *refs):
    arrived, halo = dict(zip(filter(has_halo, exchange(doms)), refs)), refs[-1]
    d = lax.axis_index("dom")
    halo[...] = jnp.zeros_like(halo)
    for k, ref in arrived.items():
        for side, step in enumerate((-1, 1)):

            @pl.when(d ^ k == d + step)
            def _():
                halo[side] = ref[2 * slots : 2 * slots + PIECES]


def couple(doms, slots, own, peer, slot, send, turned, modes, stiff, halo, *refs):
    arrived, (_, total, out, foreign, held, sems) = dict(zip(exchange(doms), refs)), refs[doms:]
    count = foreign.shape[1]
    rows = total.shape[0] // count
    d = lax.axis_index("dom")
    for k in range(doms):
        for j in range(slots):
            foreign[(d ^ k) * slots + j] = arrived[k][j]
    for side, row in enumerate((0, rows - 1)):
        near = whole(halo[side, 0], halo[side, 1])
        weight = 0.5 * (stiff[0, row : row + 1, :] + whole(halo[side, 2, 0:1], halo[side, 2, 1:2]))
        total[row * count : (row + 1) * count, :] += weight * (modes[pl.ds(row, count, stride=rows), :] - near)

    def subtract(row, term):
        part = pl.ds(pl.multiple_of(row * count, count), count)
        total[part, :] -= term

    take_back(d, count, slots, send, total, ((k, arrived[k]) for k in range(doms) if not has_halo(k)))
    for p in range(0, turned.shape[0], 2):
        first, second = (foreign[peer[0, 0, 0, q] * slots + slot[0, 0, 0, q]] for q in (p, p + 1))
        for q, term in zip((p, p + 1), pair_dot(first, second, turned[p : p + 2])):
            subtract(own[0, 0, 0, q], term)
    copies = []
    for i in range(2):
        some = range(i * count // 2, (i + 1) * count // 2)
        for m in some:
            held[m * rows : (m + 1) * rows, :] = total[pl.ds(m, rows, stride=count), :]
        part = pl.ds(some[0] * rows, len(some) * rows)
        copies.append(pltpu.make_async_copy(held.at[part], out.at[part], sems.at[i]))
        copies[-1].start()
    for copy in copies:
        copy.wait()


def exchange(doms):
    if doms == 4:
        return [3, 1, 2, 0]
    return list(range(doms))


def shards(doms, subs, modes_in, stiffness, coupling, pair_own, pair_peer, pair_slot, send_rows):
    _, count, rows, cells = modes_in.shape
    slots, pairs = send_rows.shape[-1], coupling.shape[3]
    flat = modes_in.reshape(count * rows, cells)
    inputs = (pair_own, pair_peer, pair_slot, send_rows, flat, stiffness, coupling)
    *inputs, coupling = [pltpu.with_memory_space_constraint(a, pltpu.HBM) for a in inputs]
    params = pltpu.CompilerParams(vmem_limit_bytes=32 * 1024 * 1024)
    like = jax.ShapeDtypeStruct
    indices = inputs[:4]
    *outgoing, column, blocks, modes, stiff, own, peer, slot, send = pl.pallas_call(
        functools.partial(before, doms, subs, slots, rows),
        out_shape=[like((2 * slots + PIECES * has_halo(k), count, cells), jnp.bfloat16) for k in range(doms)]
        + [
            like((1, (slots + 1) * count, cells) if subs == 2 else (2, rows, cells), jnp.float32),
            like((pairs, cells, cells), jnp.bfloat16),
            like(flat.shape, jnp.float32),
            like(stiffness.shape, jnp.float32),
        ]
        + [pltpu.SMEM(a.shape, a.dtype) for a in indices],
        in_specs=[HBM] * 7,
        out_specs=[VMEM] * (doms + 4) + [SMEM] * 4,
        scratch_shapes=[
            pltpu.VMEM((rows, count, cells), jnp.bfloat16),
            pltpu.VMEM((doms * slots, count, cells), jnp.float32),
            pltpu.SemaphoreType.DMA((len(inputs),)),
            pltpu.SemaphoreType.DMA((2,)),
        ],
        compiler_params=params,
        name="before",
    )(*inputs, coupling)
    indices = [pltpu.with_memory_space_constraint(a, pltpu.SMEM) for a in (own, peer, slot, send)]
    arrived = {}
    for k in exchange(doms):
        route = [(2 * d + h, 2 * (d ^ k) + 1 - h) for d in range(doms) for h in range(2)]
        arrived[k] = lax.ppermute(outgoing[k], ("dom", "mesh"), route)
    if subs == 1:
        columns = []
    elif subs == 2:
        columns = [lax.ppermute(column, "sub", [(0, 1), (1, 0)])]
    else:
        columns = [
            lax.ppermute(column, "sub", [(i, i + 1) for i in range(subs - 1)]),
            lax.ppermute(column, "sub", [(i + 1, i) for i in range(subs - 1)]),
        ]
    cost = pl.CostEstimate(flops=0, bytes_accessed=8 << 20, transcendentals=0)
    turned = pl.pallas_call(
        turn,
        out_shape=like(blocks.shape, blocks.dtype),
        in_specs=[VMEM],
        out_specs=VMEM,
        compiler_params=params,
        cost_estimate=cost,
        name="turn",
    )(blocks)
    picked = pl.pallas_call(
        functools.partial(pick, doms, slots),
        out_shape=like((2, PIECES, count, cells), jnp.bfloat16),
        in_specs=[VMEM] * sum(map(has_halo, range(doms))) + [ANY],
        out_specs=VMEM,
        compiler_params=params,
        name="pick",
    )(*(arrived[k] for k in exchange(doms) if has_halo(k)), turned)
    partial = pl.pallas_call(
        functools.partial(stencil, doms, subs, slots),
        out_shape=like(flat.shape, jnp.float32),
        in_specs=[SMEM, VMEM, VMEM, ANY] + [VMEM] * (sum(map(has_halo, range(doms))) + len(columns)),
        out_specs=VMEM,
        compiler_params=params,
        name="stencil",
    )(indices[3], modes, stiff, picked, *(arrived[k] for k in exchange(doms) if has_halo(k)), *columns)
    halo = lax.ppermute(picked, "mesh", [(0, 1), (1, 0)])
    _, out = pl.pallas_call(
        functools.partial(couple, doms, slots),
        out_shape=[like(partial.shape, partial.dtype)] * 2,
        in_specs=[SMEM] * 4 + [VMEM] * (5 + doms),
        out_specs=[VMEM, HBM],
        scratch_shapes=[
            pltpu.VMEM((doms * slots, count, cells), jnp.bfloat16),
            pltpu.VMEM(flat.shape, jnp.float32),
            pltpu.SemaphoreType.DMA((2,)),
        ],
        input_output_aliases={8 + doms: 0},
        compiler_params=params,
        cost_estimate=cost,
        name="couple",
    )(*indices, turned, modes, stiff, halo, *(arrived[k] for k in exchange(doms)), partial)
    return out.reshape(modes_in.shape)


def solution(mesh):
    return jax.shard_map(
        functools.partial(shards, mesh.shape["dom"], mesh.shape["sub"]),
        mesh=mesh,
        in_specs=(
            P("mesh", "copies", "dom", "sub"),
            P(("copies", "mesh"), "dom", "sub"),
            P("mesh", "dom", "sub", None, None, None),
            P("mesh", "dom", "sub", None),
            P("mesh", "dom", "sub", None),
            P("mesh", "dom", "sub", None),
            P("mesh", "dom", "sub", None, None),
        ),
        out_specs=P("mesh", "copies", "dom", "sub"),
        check_vma=False,
    )
```
